512 devices in a mesh: row: 16 (over y, core), col: 32 (over x, z).
Axes of the slice: x: 4, y: 8, z: 8, core: 2. Of those that a mesh axis runs over, the one named last changes fastest.
Arguments:
- panel_rhs: bfloat16 [2, 2048, 1024], P(None, 'row'), may hold values from -6 to 6
- diag_inverse: bfloat16 [2, 2048, 2048], P(None, 'col', 'row'), may hold values from -0.125 to 0.125
- cross_block: bfloat16 [2048, 2048], P('row', 'col'), may hold values from -0.125 to 0.125
- trail_factor: bfloat16 [16384, 2, 2048], P('row', None, 'col'), may hold values from -0.09375 to 0.09375
- trail_rhs: float32 [16384, 1024], P('row', 'col'), may hold values from -6 to 6
Outputs:
- solved: bfloat16 [2, 2048, 1024], P(None, 'col')
- trail_new: float32 [16384, 1024], P('row', 'col')
The draws below stay inside these ranges and needn't reach their ends.
All inputs are finite; a program needn't handle non-finite values.
Results may differ from the reference program's by a relative error of at most 0.015.
Values may be sent and summed in bfloat16 or wider, within the bound.
A program may use at most 64 MiB of HBM per device.

```python
import jax
import jax.numpy as jnp
from jax import lax

W = 2048
NRHS = 1024
TRAIL = 16384


def levels(own_key, extent, shards, least, top_value):
    def one(position, shards_of):
        draws = jax.random.uniform(jax.random.fold_in(jax.random.fold_in(own_key, 6), position), (shards_of,), jnp.float32, least / len(shards), top_value / len(shards))
        return jnp.repeat(jnp.exp(draws), extent[position] // shards_of).reshape((-1,) + (1,) * (len(extent) - position - 1))

    gain = one(*shards[0])
    for cut in shards[1:]:
        gain = gain * one(*cut)
    return gain


def centred(key, dims, spread, bound, split=(), dtype=jnp.bfloat16):
    entries = jax.random.normal(key, dims, jnp.float32) * spread
    if len(split) > 0:
        entries = levels(key, dims, split, -0.22, 0.18) * entries
    return jnp.clip(entries, min=-bound, max=bound).astype(dtype)


def setup_inputs(seed: int = 0) -> dict:
    key_list = jax.random.split(jax.random.key(seed), 6)
    panel_rhs = centred(key_list[0], (2, W, NRHS), 1.0, 6.0, ((1, 16),))
    diag_inverse = centred(key_list[1], (2, W, W), W ** -0.5, 0.125, ((1, 32), (2, 16)))
    cross_block = centred(key_list[2], (W, W), W ** -0.5, 0.125, ((0, 16), (1, 32)))
    trail_factor = centred(key_list[3], (TRAIL, 2, W), (2 * W) ** -0.5, 0.09375, ((0, 16), (2, 32)))
    trail_rhs = centred(key_list[4], (TRAIL, NRHS), 1.0, 6.0, ((0, 16), (1, 32)), jnp.float32)
    return dict(panel_rhs=panel_rhs, diag_inverse=diag_inverse, cross_block=cross_block, trail_factor=trail_factor, trail_rhs=trail_rhs)


def product(left, right_side):
    return jnp.dot(left.astype(jnp.float32), right_side.astype(jnp.float32), precision=lax.Precision.HIGHEST)


def reference(panel_rhs, diag_inverse, cross_block, trail_factor, trail_rhs):
    first_panel = product(diag_inverse[0], panel_rhs[0]).astype(jnp.bfloat16)
    crossed = product(cross_block, first_panel)
    reduced = (panel_rhs[1].astype(jnp.float32) - crossed).astype(jnp.bfloat16)
    second_panel = product(diag_inverse[1], reduced).astype(jnp.bfloat16)
    solved = jnp.stack([first_panel, second_panel])
    flat_factor = trail_factor.reshape(trail_factor.shape[0], 2 * W)
    update = product(flat_factor, solved.reshape(2 * W, NRHS))
    return solved, trail_rhs - update
```

```python
import functools

import jax
import jax.numpy as jnp
from jax import lax
from jax.experimental import pallas as pl
from jax.experimental.pallas import tpu as pltpu
from jax.sharding import PartitionSpec as P

MESH = pl.DeviceIdType.MESH
BF16 = jnp.bfloat16
F32 = jnp.float32


def contract_rows(left, right):
    return lax.dot_general(left, right, (((0,), (0,)), ((), ())), preferred_element_type=F32)


def contract(left, right):
    return jnp.dot(left, right, preferred_element_type=F32)


def kernel(
    R, X, Z,
    rhs, diag, cross, trail, old,
    solved, new,
    trail_all, diag_all, cross_all, partial, sent, landed, panels, cross_sent, cross_landed,
    update, update_sent, update_landed, rows_landed, spread,
    local_sem, near_send, near_recv, trail_send, trail_recv, sum_send, sum_recv,
    rows_send, rows_recv, last_send, last_recv,
):
    row, col = lax.axis_index("row"), lax.axis_index("col")
    x, z = col // Z, lax.rem(col, Z)
    bc, br = diag.shape[1:]
    nrhs = rhs.shape[2]
    share = nrhs // (X * Z)
    width = share * X
    piece = Z * bc // R

    def row_peer(d):
        return lax.rem(row + d, R)

    def x_peer(d):
        return lax.rem(x + d, X)

    def z_peer(d):
        return lax.rem(z + d + Z, Z)

    def send(src, dst, send_sem, recv_sem, where):
        copy = pltpu.make_async_remote_copy(
            src_ref=src, dst_ref=dst, send_sem=send_sem, recv_sem=recv_sem,
            device_id=where, device_id_type=MESH,
        )
        copy.start()

    def drain(ref, sem):
        pltpu.make_async_copy(ref, ref, sem).wait()

    trail_own = pltpu.make_async_copy(trail, trail_all.at[:, z], local_sem.at[0])
    trail_own.start()

    barrier = pltpu.get_barrier_semaphore()
    for d in range(1, R):
        pl.semaphore_signal(barrier, inc=1, device_id=(row_peer(d), col), device_id_type=MESH)
    for d in range(1, X):
        pl.semaphore_signal(barrier, inc=1, device_id=(row, x_peer(d) * Z + z), device_id_type=MESH)
    for d in range(1, Z):
        pl.semaphore_signal(barrier, inc=1, device_id=(row, x * Z + z_peer(d)), device_id_type=MESH)

    diag_all[0, z] = diag[0]
    diag_all[1, z] = diag[1]
    cross_all[z] = cross[...]
    source = lax.broadcasted_iota(jnp.int32, (nrhs, width), 0)
    lane = lax.broadcasted_iota(jnp.int32, (nrhs, width), 1)
    pick = (source == ((lane // share) * Z + z) * share + lane % share).astype(F32).astype(BF16)
    rhs_first = contract(rhs[0], pick).astype(BF16)
    rhs_second = contract(rhs[1], pick)
    trail_own.wait()

    pl.semaphore_wait(barrier, (R - 1) + (X - 1) + (Z - 1))

    order = sorted(range(1, Z), key=lambda d: -min(d, Z - d))
    for d in order:
        send(diag_all.at[0, z], diag_all.at[0, z], near_send.at[0], near_recv.at[0], (row, x * Z + z_peer(d)))
    for d in order:
        send(cross_all.at[z], cross_all.at[z], near_send.at[1], near_recv.at[1], (row, x * Z + z_peer(d)))
    for d in order:
        send(diag_all.at[1, z], diag_all.at[1, z], near_send.at[2], near_recv.at[2], (row, x * Z + z_peer(d)))

    half = Z // 2

    def ring_has(way, panel, step):
        return step < half or (step == half and way == panel)

    def ring_send(step):
        for panel in range(2):
            for way in range(2):
                if ring_has(way, panel, step):
                    sign = 1 - 2 * way
                    block = z_peer(-sign * (step - 1))
                    send(
                        trail_all.at[panel, block], trail_all.at[panel, block],
                        trail_send.at[way, panel, step - 1], trail_recv.at[way, panel, step - 1],
                        (row, x * Z + z_peer(sign)),
                    )

    def ring_wait(step, panels_in=(0, 1)):
        for panel in panels_in:
            for way in range(2):
                if ring_has(way, panel, step):
                    drain(trail_all.at[panel, 0], trail_recv.at[way, panel, step - 1])

    def ring_drain():
        for step in range(1, half + 1):
            for panel in range(2):
                for way in range(2):
                    if ring_has(way, panel, step):
                        drain(trail_all.at[panel, 0], trail_send.at[way, panel, step - 1])

    ring_send(1)

    def scatter(panel, right_side):
        total = contract(diag_all[panel].reshape(Z * bc, br), right_side)
        partial[...] = total
        sent[panel] = total.astype(BF16).reshape(R, piece, width)
        for d in range(1, R):
            send(sent.at[panel, row_peer(d)], landed.at[panel, d - 1], sum_send.at[panel, 0],
                 sum_recv.at[panel, 0], (row_peer(d), col))

    def gather(panel):
        drain(landed.at[panel], sum_recv.at[panel, 0])
        mine = pl.ds(pl.multiple_of(row * piece, piece), piece)
        total = partial[mine, :]
        for d in range(R - 1):
            total = total + landed[panel, d].astype(F32)
        panels[panel, mine, :] = total.astype(BF16)
        for d in range(1, R):
            send(panels.at[panel, mine, :], panels.at[panel, mine, :], sum_send.at[panel, 1],
                 sum_recv.at[panel, 1], (row_peer(d), col))

    def gathered(panel):
        drain(panels.at[panel, pl.ds(0, (R - 1) * piece), :], sum_recv.at[panel, 1])

    def spread_rows(panel):
        own = panels[panel, pl.ds(pl.multiple_of(z * bc, bc), bc), :]
        rows_landed[panel, z] = own
        for d in order:
            theirs = pl.ds(pl.multiple_of(z_peer(d) * bc, bc), bc)
            send(panels.at[panel, theirs, :], rows_landed.at[panel, z], rows_send.at[panel],
                 rows_recv.at[panel], (row, x * Z + z_peer(d)))

    def write_rows(panel):
        drain(rows_landed.at[panel, pl.ds(0, Z - 1)], rows_recv.at[panel])
        total = contract(rows_landed[panel, 0], spread[0])
        for block in range(1, Z):
            total = total + contract(rows_landed[panel, block], spread[block])
        solved[panel] = total.astype(BF16)

    drain(diag_all.at[0, pl.ds(0, Z - 1)], near_recv.at[0])
    scatter(0, rhs_first)
    for block in range(Z):
        lane = lax.broadcasted_iota(jnp.int32, (width, nrhs), 0)
        target = lax.broadcasted_iota(jnp.int32, (width, nrhs), 1)
        spread[block] = (target == ((lane // share) * Z + block) * share + lane % share).astype(F32).astype(BF16)
    gather(0)
    ring_wait(1)
    ring_send(2)
    drain(cross_all.at[pl.ds(0, Z - 1)], near_recv.at[1])
    gathered(0)

    crossed = contract_rows(cross_all[...].reshape(Z * bc, br), panels[0])
    cross_sent[...] = crossed.astype(BF16)
    for d in range(1, X):
        send(cross_sent, cross_landed.at[d - 1], last_send.at[0], last_recv.at[0],
             (row, x_peer(d) * Z + z))
    spread_rows(0)
    drain(diag_all.at[1, pl.ds(0, Z - 1)], near_recv.at[2])
    drain(cross_landed, last_recv.at[0])
    for d in range(X - 1):
        crossed = crossed + cross_landed[d].astype(F32)
    reduced = (rhs_second - crossed).astype(BF16)

    scatter(1, reduced)
    ring_wait(2)
    ring_send(3)
    write_rows(0)
    gather(1)
    ring_wait(3)
    ring_send(4)
    ring_wait(4, (0,))
    update[...] = contract_rows(panels[0], trail_all[0].reshape(Z * bc, trail.shape[2]))
    gathered(1)
    spread_rows(1)

    ring_wait(4, (1,))
    total = update[...] + contract_rows(panels[1], trail_all[1].reshape(Z * bc, trail.shape[2]))
    update[...] = total
    update_sent[...] = total.astype(BF16).reshape(X, share, trail.shape[2])
    for d in range(1, X):
        send(update_sent.at[x_peer(d)], update_landed.at[d - 1], last_send.at[1], last_recv.at[1],
             (row, x_peer(d) * Z + z))
    write_rows(1)
    total = update[pl.ds(pl.multiple_of(x * share, share), share), :]
    drain(update_landed, last_recv.at[1])
    for d in range(X - 1):
        total = total + update_landed[d].astype(F32)
    new[...] = old[...] - total

    drain(diag_all.at[0, pl.ds(0, Z - 1)], near_send.at[0])
    drain(cross_all.at[pl.ds(0, Z - 1)], near_send.at[1])
    drain(diag_all.at[1, pl.ds(0, Z - 1)], near_send.at[2])
    ring_drain()
    for panel in range(2):
        drain(landed.at[panel], sum_send.at[panel, 0])
        drain(panels.at[panel, pl.ds(0, (R - 1) * piece), :], sum_send.at[panel, 1])
        drain(rows_landed.at[panel, pl.ds(0, Z - 1)], rows_send.at[panel])
    drain(cross_landed, last_send.at[0])
    drain(update_landed, last_send.at[1])


def build(mesh, X, Z):
    R = mesh.shape["row"]

    def per_device(panel_rhs, diag_inverse, cross_block, trail_factor, trail_rhs):
        _, br, nrhs = panel_rhs.shape
        bc = diag_inverse.shape[1]
        rows = trail_factor.shape[0]
        share = nrhs // (X * Z)
        width = share * X
        piece = Z * bc // R
        vmem = pl.BlockSpec(memory_space=pltpu.VMEM)
        solved, new = pl.pallas_call(
            functools.partial(kernel, R, X, Z),
            out_shape=(
                jax.ShapeDtypeStruct((2, bc, nrhs), BF16),
                jax.ShapeDtypeStruct((share, rows), F32),
            ),
            in_specs=[vmem, vmem, vmem, pl.BlockSpec(memory_space=pl.ANY), vmem],
            out_specs=(vmem, vmem),
            scratch_shapes=[
                pltpu.VMEM((2, Z, bc, rows), BF16),
                pltpu.VMEM((2, Z, bc, br), BF16),
                pltpu.VMEM((Z, bc, br), BF16),
                pltpu.VMEM((Z * bc, width), F32),
                pltpu.VMEM((2, R, piece, width), BF16),
                pltpu.VMEM((2, R - 1, piece, width), BF16),
                pltpu.VMEM((2, Z * bc, width), BF16),
                pltpu.VMEM((br, width), BF16),
                pltpu.VMEM((X - 1, br, width), BF16),
                pltpu.VMEM((width, rows), F32),
                pltpu.VMEM((X, share, rows), BF16),
                pltpu.VMEM((X - 1, share, rows), BF16),
                pltpu.VMEM((2, Z, bc, width), BF16),
                pltpu.VMEM((Z, width, nrhs), BF16),
                pltpu.SemaphoreType.DMA((1,)),
                pltpu.SemaphoreType.DMA((3,)),
                pltpu.SemaphoreType.DMA((3,)),
                pltpu.SemaphoreType.DMA((2, 2, Z // 2)),
                pltpu.SemaphoreType.DMA((2, 2, Z // 2)),
                pltpu.SemaphoreType.DMA((2, 2)),
                pltpu.SemaphoreType.DMA((2, 2)),
                pltpu.SemaphoreType.DMA((2,)),
                pltpu.SemaphoreType.DMA((2,)),
                pltpu.SemaphoreType.DMA((2,)),
                pltpu.SemaphoreType.DMA((2,)),
            ],
            compiler_params=pltpu.CompilerParams(
                collective_id=0, has_side_effects=True, vmem_limit_bytes=40 * 1024 * 1024
            ),
        )(
            panel_rhs,
            diag_inverse,
            cross_block.T,
            jnp.transpose(trail_factor, (1, 2, 0)),
            trail_rhs.T,
        )
        return solved, new.T

    in_specs = (
        P(None, "row", None),
        P(None, "col", "row"),
        P("row", "col"),
        P("row", None, "col"),
        P("row", "col"),
    )
    out_specs = (P(None, "col", None), P("row", "col"))
    return jax.shard_map(
        per_device, mesh=mesh, in_specs=in_specs, out_specs=out_specs, check_vma=False
    )


def solution(mesh):
    return build(mesh, 4, 8)
```

```python
import functools

import jax
import jax.numpy as jnp
from jax import lax
from jax.experimental import pallas as pl
from jax.experimental.pallas import tpu as pltpu
from jax.sharding import PartitionSpec as P

MESH = pl.DeviceIdType.MESH
BF16 = jnp.bfloat16
F32 = jnp.float32


def contract_rows(left, right):
    return lax.dot_general(left, right, (((0,), (0,)), ((), ())), preferred_element_type=F32)


def contract(left, right):
    return jnp.dot(left, right, preferred_element_type=F32)


def kernel(
    R, X, Z,
    rhs_hbm, diag_hbm, cross_hbm, trail_hbm, old_hbm,
    solved, new,
    rhs, old, trail_all, diag_all, cross_all, partial, sent, landed, panels, cross_sent, cross_landed,
    update, update_sent, update_landed, rows_landed, spread, cross_turned,
    local_sem, near_send, near_recv, trail_send, trail_recv, sum_send, sum_recv,
    rows_send, rows_recv, last_send, last_recv,
):
    row, col = lax.axis_index("row"), lax.axis_index("col")
    x, z = col // Z, lax.rem(col, Z)
    bc, br = diag_hbm.shape[1:]
    nrhs = rhs_hbm.shape[2]
    rows = trail_hbm.shape[2]
    share = nrhs // (X * Z)
    width = share * X
    piece = Z * bc // R

    rings = R // 2
    y, core = row // 2, lax.rem(row, 2)
    row_steps = [
        (dy, dc)
        for dy in sorted(range(rings), key=lambda d: -min(d, rings - d))
        for dc in range(2)
        if dy or dc
    ]
    row_peers = [lax.rem(y + dy, rings) * 2 + lax.rem(core + dc, 2) for dy, dc in row_steps]
    x_steps = sorted(range(1, X), key=lambda d: -min(d, X - d))
    order = sorted(range(1, Z), key=lambda d: -min(d, Z - d))

    def x_peer(d):
        return lax.rem(x + d, X)

    def z_peer(d):
        return lax.rem(z + d + Z, Z)

    bits = share.bit_length() - 1

    def chosen(target, lane, block):
        group = lax.shift_right_logical(lane, bits)
        return (target == (group * Z + block) * share + (lane & (share - 1))).astype(F32).astype(BF16)

    def send(src, dst, send_sem, recv_sem, where):
        copy = pltpu.make_async_remote_copy(
            src_ref=src, dst_ref=dst, send_sem=send_sem, recv_sem=recv_sem,
            device_id=where, device_id_type=MESH,
        )
        copy.start()

    def drain(ref, sem):
        pltpu.make_async_copy(ref, ref, sem).wait()

    loads = [
        pltpu.make_async_copy(src, dst, local_sem.at[i])
        for i, (src, dst) in enumerate([
            (rhs_hbm, rhs), (diag_hbm, diag_all.at[:, z]), (cross_hbm, cross_all.at[z]),
            (trail_hbm, trail_all.at[:, z]), (old_hbm, old),
        ])
    ]
    for load in loads:
        load.start()

    barrier = pltpu.get_barrier_semaphore()
    for peer in row_peers:
        pl.semaphore_signal(barrier, inc=1, device_id=(peer, col), device_id_type=MESH)
    for d in x_steps:
        pl.semaphore_signal(barrier, inc=1, device_id=(row, x_peer(d) * Z + z), device_id_type=MESH)
    for d in order:
        pl.semaphore_signal(barrier, inc=1, device_id=(row, x * Z + z_peer(d)), device_id_type=MESH)

    source = lax.broadcasted_iota(jnp.int32, (nrhs, width), 0)
    lane = lax.broadcasted_iota(jnp.int32, (nrhs, width), 1)
    pick = chosen(source, lane, z)
    loads[0].wait()
    rhs_first = contract(rhs[0], pick).astype(BF16)
    rhs_second = contract(rhs[1], pick)
    for load in loads[1:]:
        load.wait()

    pl.semaphore_wait(barrier, (R - 1) + (X - 1) + (Z - 1))

    for d in order:
        send(diag_all.at[0, z], diag_all.at[0, z], near_send.at[0], near_recv.at[0], (row, x * Z + z_peer(d)))
    for d in order:
        send(cross_all.at[z], cross_all.at[z], near_send.at[1], near_recv.at[1], (row, x * Z + z_peer(d)))
    for d in order:
        send(diag_all.at[1, z], diag_all.at[1, z], near_send.at[2], near_recv.at[2], (row, x * Z + z_peer(d)))

    half = Z // 2

    def ring_has(way, panel, step):
        return step < half or (step == half and way == panel)

    def ring_send(step):
        for panel in range(2):
            for way in range(2):
                if ring_has(way, panel, step):
                    sign = 1 - 2 * way
                    block = z_peer(-sign * (step - 1))
                    send(
                        trail_all.at[panel, block], trail_all.at[panel, block],
                        trail_send.at[way, panel, step - 1], trail_recv.at[way, panel, step - 1],
                        (row, x * Z + z_peer(sign)),
                    )

    def ring_wait(step, panels_in=(0, 1)):
        for panel in panels_in:
            for way in range(2):
                if ring_has(way, panel, step):
                    drain(trail_all.at[panel, 0], trail_recv.at[way, panel, step - 1])

    def ring_drain():
        for step in range(1, half + 1):
            for panel in range(2):
                for way in range(2):
                    if ring_has(way, panel, step):
                        drain(trail_all.at[panel, 0], trail_send.at[way, panel, step - 1])

    ring_send(1)

    def scatter(panel, right_side):
        total = contract(diag_all[panel].reshape(Z * bc, br), right_side)
        partial[...] = total
        sent[panel] = total.astype(BF16).reshape(R, piece, width)
        for slot, peer in enumerate(row_peers):
            send(sent.at[panel, peer], landed.at[panel, slot], sum_send.at[panel, 0],
                 sum_recv.at[panel, 0], (peer, col))

    def gather(panel):
        drain(landed.at[panel], sum_recv.at[panel, 0])
        mine = pl.ds(pl.multiple_of(row * piece, piece), piece)
        total = partial[mine, :]
        for d in range(R - 1):
            total = total + landed[panel, d].astype(F32)
        panels[panel, mine, :] = total.astype(BF16)
        for peer in row_peers:
            send(panels.at[panel, mine, :], panels.at[panel, mine, :], sum_send.at[panel, 1],
                 sum_recv.at[panel, 1], (peer, col))

    def gathered(panel):
        drain(panels.at[panel, pl.ds(0, (R - 1) * piece), :], sum_recv.at[panel, 1])

    def spread_rows(panel):
        own = panels[panel, pl.ds(pl.multiple_of(z * bc, bc), bc), :]
        rows_landed[panel, z] = own
        for d in order:
            theirs = pl.ds(pl.multiple_of(z_peer(d) * bc, bc), bc)
            send(panels.at[panel, theirs, :], rows_landed.at[panel, z], rows_send.at[panel],
                 rows_recv.at[panel], (row, x * Z + z_peer(d)))

    def write_rows(panel):
        drain(rows_landed.at[panel, pl.ds(0, Z - 1)], rows_recv.at[panel])
        total = contract(rows_landed[panel, 0], spread[0])
        for block in range(1, Z):
            total = total + contract(rows_landed[panel, block], spread[block])
        solved[panel] = total.astype(BF16)

    drain(diag_all.at[0, pl.ds(0, Z - 1)], near_recv.at[0])
    scatter(0, rhs_first)
    lane = lax.broadcasted_iota(jnp.int32, (width, nrhs), 0)
    target = lax.broadcasted_iota(jnp.int32, (width, nrhs), 1)

    def fill(block, _):
        spread[block] = chosen(target, lane, block)
        return 0

    lax.fori_loop(0, Z, fill, 0)
    gather(0)
    ring_wait(1)
    ring_send(2)
    drain(cross_all.at[pl.ds(0, Z - 1)], near_recv.at[1])
    cross_turned[...] = cross_all[...].reshape(Z * bc, br).T
    gathered(0)

    crossed = contract(cross_turned[...], panels[0])
    cross_sent[...] = crossed.astype(BF16)
    for d in x_steps:
        send(cross_sent, cross_landed.at[d - 1], last_send.at[0], last_recv.at[0],
             (row, x_peer(d) * Z + z))
    spread_rows(0)
    drain(diag_all.at[1, pl.ds(0, Z - 1)], near_recv.at[2])
    drain(cross_landed, last_recv.at[0])
    for d in range(X - 1):
        crossed = crossed + cross_landed[d].astype(F32)
    reduced = (rhs_second - crossed).astype(BF16)

    scatter(1, reduced)
    ring_wait(2)
    ring_send(3)
    write_rows(0)
    gather(1)
    ring_wait(3)
    ring_send(4)
    ring_wait(4, (0,))
    update[...] = contract_rows(panels[0], trail_all[0].reshape(Z * bc, rows))
    gathered(1)
    spread_rows(1)

    ring_wait(4, (1,))
    total = update[...] + contract_rows(panels[1], trail_all[1].reshape(Z * bc, rows))
    update[...] = total
    update_sent[...] = total.astype(BF16).reshape(X, share, rows)
    for d in x_steps:
        send(update_sent.at[x_peer(d)], update_landed.at[d - 1], last_send.at[1], last_recv.at[1],
             (row, x_peer(d) * Z + z))
    write_rows(1)
    total = update[pl.ds(pl.multiple_of(x * share, share), share), :]
    drain(update_landed, last_recv.at[1])
    for d in range(X - 1):
        total = total + update_landed[d].astype(F32)
    new[...] = old[...] - total

    drain(diag_all.at[0, pl.ds(0, Z - 1)], near_send.at[0])
    drain(cross_all.at[pl.ds(0, Z - 1)], near_send.at[1])
    drain(diag_all.at[1, pl.ds(0, Z - 1)], near_send.at[2])
    ring_drain()
    for panel in range(2):
        drain(landed.at[panel], sum_send.at[panel, 0])
        drain(panels.at[panel, pl.ds(0, (R - 1) * piece), :], sum_send.at[panel, 1])
        drain(rows_landed.at[panel, pl.ds(0, Z - 1)], rows_send.at[panel])
    drain(cross_landed, last_send.at[0])
    drain(update_landed, last_send.at[1])


def build(mesh, X, Z):
    R = mesh.shape["row"]

    def per_device(panel_rhs, diag_inverse, cross_block, trail_factor, trail_rhs):
        _, br, nrhs = panel_rhs.shape
        bc = diag_inverse.shape[1]
        rows = trail_factor.shape[0]
        share = nrhs // (X * Z)
        width = share * X
        piece = Z * bc // R
        vmem = pl.BlockSpec(memory_space=pltpu.VMEM)
        solved, new = pl.pallas_call(
            functools.partial(kernel, R, X, Z),
            out_shape=(
                jax.ShapeDtypeStruct((2, bc, nrhs), BF16),
                jax.ShapeDtypeStruct((share, rows), F32),
            ),
            in_specs=[pl.BlockSpec(memory_space=pltpu.HBM)] * 5,
            out_specs=(vmem, vmem),
            scratch_shapes=[
                pltpu.VMEM((2, br, nrhs), BF16),
                pltpu.VMEM((share, rows), F32),
                pltpu.VMEM((2, Z, bc, rows), BF16),
                pltpu.VMEM((2, Z, bc, br), BF16),
                pltpu.VMEM((Z, bc, br), BF16),
                pltpu.VMEM((Z * bc, width), F32),
                pltpu.VMEM((2, R, piece, width), BF16),
                pltpu.VMEM((2, R - 1, piece, width), BF16),
                pltpu.VMEM((2, Z * bc, width), BF16),
                pltpu.VMEM((br, width), BF16),
                pltpu.VMEM((X - 1, br, width), BF16),
                pltpu.VMEM((width, rows), F32),
                pltpu.VMEM((X, share, rows), BF16),
                pltpu.VMEM((X - 1, share, rows), BF16),
                pltpu.VMEM((2, Z, bc, width), BF16),
                pltpu.VMEM((Z, width, nrhs), BF16),
                pltpu.VMEM((br, Z * bc), BF16),
                pltpu.SemaphoreType.DMA((5,)),
                pltpu.SemaphoreType.DMA((3,)),
                pltpu.SemaphoreType.DMA((3,)),
                pltpu.SemaphoreType.DMA((2, 2, Z // 2)),
                pltpu.SemaphoreType.DMA((2, 2, Z // 2)),
                pltpu.SemaphoreType.DMA((2, 2)),
                pltpu.SemaphoreType.DMA((2, 2)),
                pltpu.SemaphoreType.DMA((2,)),
                pltpu.SemaphoreType.DMA((2,)),
                pltpu.SemaphoreType.DMA((2,)),
                pltpu.SemaphoreType.DMA((2,)),
            ],
            compiler_params=pltpu.CompilerParams(
                collective_id=0, has_side_effects=True, vmem_limit_bytes=63 * 1024 * 1024
            ),
        )(
            panel_rhs,
            diag_inverse,
            cross_block.T,
            jnp.transpose(trail_factor, (1, 2, 0)),
            trail_rhs.T,
        )
        return solved, new.T

    in_specs = (
        P(None, "row", None),
        P(None, "col", "row"),
        P("row", "col"),
        P("row", None, "col"),
        P("row", "col"),
    )
    out_specs = (P(None, "col", None), P("row", "col"))
    return jax.shard_map(
        per_device, mesh=mesh, in_specs=in_specs, out_specs=out_specs, check_vma=False
    )


def solution(mesh):
    return build(mesh, 4, 8)
```

```python
import functools

import jax
import jax.numpy as jnp
from jax import lax
from jax.experimental import pallas as pl
from jax.experimental.pallas import tpu as pltpu
from jax.sharding import PartitionSpec as P

MESH = pl.DeviceIdType.MESH
BF16 = jnp.bfloat16
F32 = jnp.float32


def contract_rows(left, right):
    return lax.dot_general(left, right, (((0,), (0,)), ((), ())), preferred_element_type=F32)


def contract(left, right):
    return jnp.dot(left, right, preferred_element_type=F32)


def kernel(
    R, X, Z,
    rhs_hbm, diag_hbm, cross_hbm, trail_hbm, old_hbm,
    solved, new,
    rhs, old, trail_all, diag_first, diag_all, cross_all, partial, sent, landed, panels, cross_sent, cross_landed,
    update, update_sent, update_landed, rows_landed, cross_turned, first_sent, first_landed, first_own, first_piece, first_rows,
    local_sem, near_send, near_recv, trail_send, trail_recv, sum_send, sum_recv,
    rows_send, rows_recv, last_send, last_recv, first_send, first_recv,
):
    row, col = lax.axis_index("row"), lax.axis_index("col")
    x, z = col // Z, lax.rem(col, Z)
    bc, br = diag_hbm.shape[1:]
    nrhs = rhs_hbm.shape[2]
    rows = trail_hbm.shape[2]
    share = nrhs // (X * Z)
    width = share * X
    piece = Z * bc // R

    rings = R // 2
    y, core = row // 2, lax.rem(row, 2)
    row_steps = [
        (dy, dc)
        for dy in sorted(range(rings), key=lambda d: -min(d, rings - d))
        for dc in range(2)
        if dy or dc
    ]
    row_peers = [lax.rem(y + dy, rings) * 2 + lax.rem(core + dc, 2) for dy, dc in row_steps]
    x_steps = sorted(range(1, X), key=lambda d: -min(d, X - d))
    order = sorted(range(1, Z), key=lambda d: -min(d, Z - d))

    def x_peer(d):
        return lax.rem(x + d, X)

    def z_peer(d):
        return lax.rem(z + d + Z, Z)

    sets = Z // 2
    slabs = R // sets
    slab = bc // slabs
    my_set, my_slab = lax.rem(row, sets), row // sets
    first_peers = [row] + row_peers
    bits = share.bit_length() - 1

    def chosen(target, lane, block):
        group = lax.shift_right_logical(lane, bits)
        return (target == (group * Z + block) * share + (lane & (share - 1))).astype(F32).astype(BF16)

    def send(src, dst, send_sem, recv_sem, where):
        copy = pltpu.make_async_remote_copy(
            src_ref=src, dst_ref=dst, send_sem=send_sem, recv_sem=recv_sem,
            device_id=where, device_id_type=MESH,
        )
        copy.start()

    def drain(ref, sem):
        pltpu.make_async_copy(ref, ref, sem).wait()

    loads = [
        pltpu.make_async_copy(src, dst, local_sem.at[i])
        for i, (src, dst) in enumerate([
            (rhs_hbm, rhs), (diag_hbm.at[0], diag_first), (diag_hbm.at[1], diag_all.at[z]), (cross_hbm, cross_all.at[z]),
            (trail_hbm, trail_all.at[:, z]), (old_hbm, old),
        ])
    ]
    for load in loads:
        load.start()

    barrier = pltpu.get_barrier_semaphore()
    for peer in row_peers:
        pl.semaphore_signal(barrier, inc=1, device_id=(peer, col), device_id_type=MESH)
    for d in x_steps:
        pl.semaphore_signal(barrier, inc=1, device_id=(row, x_peer(d) * Z + z), device_id_type=MESH)
    for d in order:
        pl.semaphore_signal(barrier, inc=1, device_id=(row, x * Z + z_peer(d)), device_id_type=MESH)
    for block in range(Z):
        for index in range(slabs):
            giver = index * sets + lax.rem(z, sets)

            @pl.when(jnp.logical_or(giver != row, z != block))
            def _():
                pl.semaphore_signal(barrier, inc=1, device_id=(giver, x * Z + block), device_id_type=MESH)

    at_home = (my_set == lax.rem(z, sets)).astype(jnp.int32)

    loads[0].wait()
    place = lax.shift_right_logical(lax.broadcasted_iota(jnp.int32, (br, width), 1), bits)
    tiles = [rhs[0, :, tile * width:(tile + 1) * width].astype(F32) for tile in range(Z)]
    loads[1].wait()
    for block in range(Z):
        mixed = None
        for group in range(X):
            tile, q = divmod(group * Z + block, X)
            shift = (group - q) % X * share
            moved = pltpu.roll(tiles[tile], shift, 1) if shift else tiles[tile]
            mixed = moved if mixed is None else jnp.where(place == group, moved, mixed)
        product = contract(diag_first[...], mixed.astype(BF16))
        rounded = product.astype(BF16)
        for index in range(slabs):
            first_own[index * sets + block % sets, block // sets] = product[index * slab:(index + 1) * slab]
            first_sent[index * sets + block % sets, block // sets] = rounded[index * slab:(index + 1) * slab]

    pl.semaphore_wait(barrier, (R - 1) + (X - 1) + (Z - 1) + 2 * R - at_home)

    for slot, peer in enumerate(row_peers):
        send(first_sent.at[peer], first_landed.at[slot], first_send.at[0], first_recv.at[0], (peer, col))
    for load in loads[2:]:
        load.wait()
    for d in (2, -2, 1, -1):
        for which, buffer in enumerate((cross_all, diag_all)):
            send(buffer.at[z], buffer.at[z], near_send.at[0], near_recv.at[0 if abs(d) == 2 else 1 + which],
                 (row, x * Z + z_peer(d)))

    def pass_on():
        drain(cross_all.at[pl.ds(0, 4)], near_recv.at[0])
        for which, buffer in enumerate((cross_all, diag_all)):
            for sign in (1, -1):
                block = z_peer(-2 * sign)
                part = pl.ds(0 if sign == 1 else bc // 2, bc // 2)
                send(buffer.at[block], buffer.at[block], near_send.at[0], near_recv.at[1 + which],
                     (row, x * Z + z_peer(sign)))
                send(buffer.at[block, part, :], buffer.at[block, part, :], near_send.at[0], near_recv.at[1 + which],
                     (row, x * Z + z_peer(2 * sign)))

    half = Z // 2

    def ring_has(way, panel, step):
        return step < half or (step == half and way == panel)

    def ring_send(step, panel, way):
        if ring_has(way, panel, step):
            sign = 1 - 2 * way
            block = z_peer(-sign * (step - 1))
            send(
                trail_all.at[panel, block], trail_all.at[panel, block],
                trail_send.at[way, panel, step - 1], trail_recv.at[way, panel, step - 1],
                (row, x * Z + z_peer(sign)),
            )

    def ring_wait(step, panel, way):
        if ring_has(way, panel, step):
            drain(trail_all.at[panel, 0], trail_recv.at[way, panel, step - 1])

    def ring_pass(step):
        for panel in range(2):
            for way in range(2):
                ring_wait(step, panel, way)
                ring_send(step + 1, panel, way)

    def ring_drain():
        for step in range(1, half + 1):
            for panel in range(2):
                for way in range(2):
                    if ring_has(way, panel, step):
                        drain(trail_all.at[panel, 0], trail_send.at[way, panel, step - 1])

    for panel in range(2):
        for way in range(2):
            ring_send(1, panel, way)

    def scatter(panel, right_side):
        total = contract(diag_all[...].reshape(Z * bc, br), right_side)
        partial[...] = total
        sent[...] = total.astype(BF16).reshape(R, piece, width)
        for slot, peer in enumerate(row_peers):
            send(sent.at[peer], landed.at[slot], sum_send.at[0],
                 sum_recv.at[0], (peer, col))

    def gather(panel):
        drain(landed, sum_recv.at[0])
        mine = pl.ds(pl.multiple_of(row * piece, piece), piece)
        total = partial[mine, :]
        for d in range(R - 1):
            total = total + landed[d].astype(F32)
        panels[panel, mine, :] = total.astype(BF16)
        for peer in row_peers:
            send(panels.at[panel, mine, :], panels.at[panel, mine, :], sum_send.at[1],
                 sum_recv.at[1], (peer, col))

    def gathered(panel):
        drain(panels.at[panel, pl.ds(0, (R - 1) * piece), :], sum_recv.at[1])

    def spread_rows(panel):
        own = panels[panel, pl.ds(pl.multiple_of(z * bc, bc), bc), :]
        rows_landed[z] = own
        for d in order:
            theirs = pl.ds(pl.multiple_of(z_peer(d) * bc, bc), bc)
            send(panels.at[panel, theirs, :], rows_landed.at[z], rows_send.at[0],
                 rows_recv.at[0], (row, x * Z + z_peer(d)))

    def write_rows(panel, blocks):
        place = lax.shift_right_logical(lax.broadcasted_iota(jnp.int32, (bc, width), 1), bits)
        for tile in range(Z):
            group, first = divmod(tile * X, Z)
            out = None
            for q in range(X):
                shift = (q - group) % X * share
                moved = pltpu.roll(blocks[first + q], shift, 1) if shift else blocks[first + q]
                out = moved if out is None else jnp.where(place == q, moved, out)
            solved[panel, :, tile * width:(tile + 1) * width] = out.astype(BF16)

    source = lax.broadcasted_iota(jnp.int32, (nrhs, width), 0)
    lane = lax.broadcasted_iota(jnp.int32, (nrhs, width), 1)
    rhs_second = contract(rhs[1], chosen(source, lane, z))
    drain(first_landed, first_recv.at[0])
    total = first_own[row]
    for slot in range(R - 1):
        total = total + first_landed[slot].astype(F32)
    first_piece[...] = total.astype(BF16)
    first_place = pl.ds(pl.multiple_of(z * bc + my_slab * slab, slab), slab)
    for which, peer in enumerate([*row_peers, row]):
        for side in range(2):
            block = my_set + side * sets
            target = panels.at[0, first_place, :]
            if which < R - 1:
                send(first_piece.at[side], target, first_send.at[1], first_recv.at[1], (peer, x * Z + block))
            else:
                @pl.when(block != z)
                def _():
                    send(first_piece.at[side], target, first_send.at[1], first_recv.at[1], (row, x * Z + block))

                @pl.when(block == z)
                def _():
                    pltpu.make_async_copy(first_piece.at[side], target, first_recv.at[1]).start()
    first_rows[row] = first_piece[...]
    pass_on()
    for peer in row_peers:
        send(first_piece, first_rows.at[row], first_send.at[2], first_recv.at[2], (peer, col))
    ring_pass(1)
    drain(cross_all.at[pl.ds(0, Z - 3)], near_recv.at[1])
    cross_turned[...] = cross_all[...].reshape(Z * bc, br).T
    drain(panels.at[0], first_recv.at[1])

    crossed = contract(cross_turned[...], panels[0])
    cross_sent[...] = crossed.astype(BF16)
    for d in x_steps:
        send(cross_sent, cross_landed.at[d - 1], last_send.at[0], last_recv.at[0],
             (row, x_peer(d) * Z + z))
    if half > 2:
        ring_pass(2)
    drain(diag_all.at[pl.ds(0, Z - 3)], near_recv.at[2])
    drain(cross_landed, last_recv.at[0])
    for d in range(X - 1):
        crossed = crossed + cross_landed[d].astype(F32)
    reduced = (rhs_second - crossed).astype(BF16)

    scatter(1, reduced)
    for step in range(3, half):
        ring_pass(step)
    gather(1)
    ring_wait(half, 0, 0)
    update[...] = contract_rows(panels[0], trail_all[0].reshape(Z * bc, rows))
    gathered(1)
    spread_rows(1)

    ring_wait(half, 1, 1)
    total = update[...] + contract_rows(panels[1], trail_all[1].reshape(Z * bc, rows))
    update[...] = total
    update_sent[...] = total.astype(BF16).reshape(X, share, rows)
    for d in x_steps:
        send(update_sent.at[x_peer(d)], update_landed.at[d - 1], last_send.at[1], last_recv.at[1],
             (row, x_peer(d) * Z + z))
    drain(first_rows.at[pl.ds(0, R - 1)], first_recv.at[2])
    write_rows(0, [
        jnp.concatenate([first_rows[index * sets + block % sets, block // sets].astype(F32) for index in range(slabs)], axis=0)
        for block in range(Z)
    ])
    total = update[pl.ds(pl.multiple_of(x * share, share), share), :]
    drain(update_landed, last_recv.at[1])
    for d in range(X - 1):
        total = total + update_landed[d].astype(F32)
    new[...] = old[...] - total
    drain(rows_landed.at[pl.ds(0, Z - 1)], rows_recv.at[0])
    write_rows(1, [rows_landed[block].astype(F32) for block in range(Z)])

    drain(first_landed, first_send.at[0])
    drain(panels.at[0, pl.ds(0, (R - 1) * 2 * slab), :], first_send.at[1])
    for side in range(2):
        @pl.when(my_set + side * sets != z)
        def _():
            drain(first_piece.at[side], first_send.at[1])
    drain(first_rows.at[pl.ds(0, R - 1)], first_send.at[2])
    for buffer in (cross_all, diag_all):
        drain(buffer.at[pl.ds(0, Z - 1)], near_send.at[0])
    ring_drain()
    drain(landed, sum_send.at[0])
    drain(panels.at[1, pl.ds(0, (R - 1) * piece), :], sum_send.at[1])
    drain(rows_landed.at[pl.ds(0, Z - 1)], rows_send.at[0])
    drain(cross_landed, last_send.at[0])
    drain(update_landed, last_send.at[1])


def build(mesh, X, Z):
    R = mesh.shape["row"]

    def per_device(panel_rhs, diag_inverse, cross_block, trail_factor, trail_rhs):
        _, br, nrhs = panel_rhs.shape
        bc = diag_inverse.shape[1]
        rows = trail_factor.shape[0]
        share = nrhs // (X * Z)
        width = share * X
        piece = Z * bc // R
        slab = bc // (R // (Z // 2))
        vmem = pl.BlockSpec(memory_space=pltpu.VMEM)
        solved, new = pl.pallas_call(
            functools.partial(kernel, R, X, Z),
            out_shape=(
                jax.ShapeDtypeStruct((2, bc, nrhs), BF16),
                jax.ShapeDtypeStruct((share, rows), F32),
            ),
            in_specs=[pl.BlockSpec(memory_space=pltpu.HBM)] * 5,
            out_specs=(vmem, vmem),
            scratch_shapes=[
                pltpu.VMEM((2, br, nrhs), BF16),
                pltpu.VMEM((share, rows), F32),
                pltpu.VMEM((2, Z, bc, rows), BF16),
                pltpu.VMEM((bc, br), BF16),
                pltpu.VMEM((Z, bc, br), BF16),
                pltpu.VMEM((Z, bc, br), BF16),
                pltpu.VMEM((Z * bc, width), F32),
                pltpu.VMEM((R, piece, width), BF16),
                pltpu.VMEM((R - 1, piece, width), BF16),
                pltpu.VMEM((2, Z * bc, width), BF16),
                pltpu.VMEM((br, width), BF16),
                pltpu.VMEM((X - 1, br, width), BF16),
                pltpu.VMEM((width, rows), F32),
                pltpu.VMEM((X, share, rows), BF16),
                pltpu.VMEM((X - 1, share, rows), BF16),
                pltpu.VMEM((Z, bc, width), BF16),
                pltpu.VMEM((br, Z * bc), BF16),
                pltpu.VMEM((R, 2, slab, width), BF16),
                pltpu.VMEM((R - 1, 2, slab, width), BF16),
                pltpu.VMEM((R, 2, slab, width), F32),
                pltpu.VMEM((2, slab, width), BF16),
                pltpu.VMEM((R, 2, slab, width), BF16),
                pltpu.SemaphoreType.DMA((6,)),
                pltpu.SemaphoreType.DMA((1,)),
                pltpu.SemaphoreType.DMA((3,)),
                pltpu.SemaphoreType.DMA((2, 2, Z // 2)),
                pltpu.SemaphoreType.DMA((2, 2, Z // 2)),
                pltpu.SemaphoreType.DMA((2,)),
                pltpu.SemaphoreType.DMA((2,)),
                pltpu.SemaphoreType.DMA((1,)),
                pltpu.SemaphoreType.DMA((1,)),
                pltpu.SemaphoreType.DMA((2,)),
                pltpu.SemaphoreType.DMA((2,)),
                pltpu.SemaphoreType.DMA((3,)),
                pltpu.SemaphoreType.DMA((3,)),
            ],
            compiler_params=pltpu.CompilerParams(
                collective_id=0, has_side_effects=True, vmem_limit_bytes=63 * 1024 * 1024
            ),
        )(
            panel_rhs,
            diag_inverse,
            cross_block.T,
            jnp.transpose(trail_factor, (1, 2, 0)),
            trail_rhs.T,
        )
        return solved, new.T

    in_specs = (
        P(None, "row", None),
        P(None, "col", "row"),
        P("row", "col"),
        P("row", None, "col"),
        P("row", "col"),
    )
    out_specs = (P(None, "col", None), P("row", "col"))
    return jax.shard_map(
        per_device, mesh=mesh, in_specs=in_specs, out_specs=out_specs, check_vma=False
    )


def solution(mesh):
    return build(mesh, 4, 8)
```

```python
import functools

import jax
import jax.numpy as jnp
from jax import lax
from jax.experimental import pallas as pl
from jax.experimental.pallas import tpu as pltpu
from jax.sharding import PartitionSpec as P

MESH = pl.DeviceIdType.MESH
BF16 = jnp.bfloat16
F32 = jnp.float32


def contract_rows(left, right):
    return lax.dot_general(left, right, (((0,), (0,)), ((), ())), preferred_element_type=F32)


def contract(left, right):
    return jnp.dot(left, right, preferred_element_type=F32)


def kernel(
    R, X, Z,
    rhs_hbm, diag_hbm, cross_hbm, trail_hbm, old_hbm,
    solved, new,
    rhs, old, trail_all, diag_first, diag_all, cross_all, partial, sent, landed, panels, cross_sent, cross_landed,
    update, update_sent, update_landed, rows_landed, cross_turned, first_sent, first_landed, first_own, first_piece, first_rows,
    local_sem, near_send, near_recv, trail_send, trail_recv, sum_send, sum_recv,
    rows_send, rows_recv, last_send, last_recv, first_send, first_recv,
):
    row, col = lax.axis_index("row"), lax.axis_index("col")
    x, z = col // Z, lax.rem(col, Z)
    bc, br = diag_hbm.shape[1:]
    nrhs = rhs_hbm.shape[2]
    rows = trail_hbm.shape[2]
    share = nrhs // (X * Z)
    width = share * X
    piece = Z * bc // R

    rings = R // 2
    y, core = row // 2, lax.rem(row, 2)
    row_steps = [
        (dy, dc)
        for dy in sorted(range(rings), key=lambda d: -min(d, rings - d))
        for dc in range(2)
        if dy or dc
    ]
    row_peers = [lax.rem(y + dy, rings) * 2 + lax.rem(core + dc, 2) for dy, dc in row_steps]
    x_steps = sorted(range(1, X), key=lambda d: -min(d, X - d))
    order = sorted(range(1, Z), key=lambda d: -min(d, Z - d))

    def x_peer(d):
        return lax.rem(x + d, X)

    def z_peer(d):
        return lax.rem(z + d + Z, Z)

    sets = Z // 2
    slabs = R // sets
    slab = bc // slabs
    my_set, my_slab = lax.rem(row, sets), row // sets
    first_peers = [row] + row_peers
    bits = share.bit_length() - 1

    def chosen(target, lane, block):
        group = lax.shift_right_logical(lane, bits)
        return (target == (group * Z + block) * share + (lane & (share - 1))).astype(F32).astype(BF16)

    def send(src, dst, send_sem, recv_sem, where):
        copy = pltpu.make_async_remote_copy(
            src_ref=src, dst_ref=dst, send_sem=send_sem, recv_sem=recv_sem,
            device_id=where, device_id_type=MESH,
        )
        copy.start()

    def drain(ref, sem):
        pltpu.make_async_copy(ref, ref, sem).wait()

    barrier = pltpu.get_barrier_semaphore()
    for d in order:
        for index in range(slabs):
            giver = index * sets + lax.rem(z, sets)
            pl.semaphore_signal(barrier, inc=1, device_id=(giver, x * Z + z_peer(d)), device_id_type=MESH)
    for d in order:
        pl.semaphore_signal(barrier, inc=1, device_id=(row, x * Z + z_peer(d)), device_id_type=MESH)
    for peer in row_peers:
        pl.semaphore_signal(barrier, inc=1, device_id=(peer, col), device_id_type=MESH)
    for d in x_steps:
        pl.semaphore_signal(barrier, inc=1, device_id=(row, x_peer(d) * Z + z), device_id_type=MESH)
    loads = [
        pltpu.make_async_copy(src, dst, local_sem.at[i])
        for i, (src, dst) in enumerate([
            (rhs_hbm, rhs), (diag_hbm.at[0], diag_first), (diag_hbm.at[1], diag_all.at[z]), (cross_hbm, cross_all.at[z]),
            (trail_hbm, trail_all.at[:, z]), (old_hbm, old),
        ])
    ]
    for load in loads:
        load.start()
    at_home = (my_set == lax.rem(z, sets)).astype(jnp.int32)

    loads[0].wait()
    place = lax.shift_right_logical(lax.broadcasted_iota(jnp.int32, (br, width), 1), bits)
    tiles = [rhs[0, :, tile * width:(tile + 1) * width].astype(F32) for tile in range(Z)]
    loads[1].wait()
    for block in range(Z):
        mixed = None
        for group in range(X):
            tile, q = divmod(group * Z + block, X)
            shift = (group - q) % X * share
            moved = pltpu.roll(tiles[tile], shift, 1) if shift else tiles[tile]
            mixed = moved if mixed is None else jnp.where(place == group, moved, mixed)
        product = contract(diag_first[...], mixed.astype(BF16))
        rounded = product.astype(BF16)
        for index in range(slabs):
            first_own[index * sets + block % sets, block // sets] = product[index * slab:(index + 1) * slab]
            first_sent[index * sets + block % sets, block // sets] = rounded[index * slab:(index + 1) * slab]

    pl.semaphore_wait(barrier, (R - 1) + (X - 1) + (Z - 1) + (2 - at_home) * R)

    for slot, peer in enumerate(row_peers):
        send(first_sent.at[peer], first_landed.at[slot], first_send.at[0], first_recv.at[0], (peer, col))
    for load in loads[2:]:
        load.wait()
    for d in (2, -2, 1, -1):
        for which, buffer in enumerate((cross_all, diag_all)):
            send(buffer.at[z], buffer.at[z], near_send.at[0], near_recv.at[0 if abs(d) == 2 else 1 + which],
                 (row, x * Z + z_peer(d)))

    def pass_on():
        drain(cross_all.at[pl.ds(0, 4)], near_recv.at[0])
        for which, buffer in enumerate((cross_all, diag_all)):
            for sign in (1, -1):
                block = z_peer(-2 * sign)
                part = pl.ds(0 if sign == 1 else bc // 2, bc // 2)
                send(buffer.at[block], buffer.at[block], near_send.at[0], near_recv.at[1 + which],
                     (row, x * Z + z_peer(sign)))
                send(buffer.at[block, part, :], buffer.at[block, part, :], near_send.at[0], near_recv.at[1 + which],
                     (row, x * Z + z_peer(2 * sign)))

    half = Z // 2

    def ring_has(way, panel, step):
        return step < half or (step == half and way == panel)

    def ring_send(step, panel, way):
        if ring_has(way, panel, step):
            sign = 1 - 2 * way
            block = z_peer(-sign * (step - 1))
            send(
                trail_all.at[panel, block], trail_all.at[panel, block],
                trail_send.at[way, panel, step - 1], trail_recv.at[way, panel, step - 1],
                (row, x * Z + z_peer(sign)),
            )

    def ring_wait(step, panel, way):
        if ring_has(way, panel, step):
            drain(trail_all.at[panel, 0], trail_recv.at[way, panel, step - 1])

    def ring_pass(step, which=(0, 1)):
        for panel in which:
            for way in range(2):
                ring_wait(step, panel, way)
                ring_send(step + 1, panel, way)

    def ring_drain():
        for step in range(1, half + 1):
            for panel in range(2):
                for way in range(2):
                    if ring_has(way, panel, step):
                        drain(trail_all.at[panel, 0], trail_send.at[way, panel, step - 1])

    for panel in range(2):
        for way in range(2):
            ring_send(1, panel, way)

    def scatter(panel, right_side):
        total = contract(diag_all[...].reshape(Z * bc, br), right_side)
        partial[...] = total
        sent[...] = total.astype(BF16).reshape(R, piece, width)
        for slot, peer in enumerate(row_peers):
            send(sent.at[peer], landed.at[slot], sum_send.at[0],
                 sum_recv.at[0], (peer, col))

    def gather(panel):
        drain(landed, sum_recv.at[0])
        mine = pl.ds(pl.multiple_of(row * piece, piece), piece)
        total = partial[mine, :]
        for d in range(R - 1):
            total = total + landed[d].astype(F32)
        panels[panel, mine, :] = total.astype(BF16)
        for peer in row_peers:
            send(panels.at[panel, mine, :], panels.at[panel, mine, :], sum_send.at[1],
                 sum_recv.at[1], (peer, col))

    def gathered(panel):
        drain(panels.at[panel, pl.ds(0, (R - 1) * piece), :], sum_recv.at[1])

    def spread_rows(panel):
        own = panels[panel, pl.ds(pl.multiple_of(z * bc, bc), bc), :]
        rows_landed[z] = own
        for d in order:
            theirs = pl.ds(pl.multiple_of(z_peer(d) * bc, bc), bc)
            send(panels.at[panel, theirs, :], rows_landed.at[z], rows_send.at[0],
                 rows_recv.at[0], (row, x * Z + z_peer(d)))

    def write_rows(panel, blocks):
        place = lax.shift_right_logical(lax.broadcasted_iota(jnp.int32, (bc, width), 1), bits)
        for tile in range(Z):
            group, first = divmod(tile * X, Z)
            out = None
            for q in range(X):
                shift = (q - group) % X * share
                moved = pltpu.roll(blocks[first + q], shift, 1) if shift else blocks[first + q]
                out = moved if out is None else jnp.where(place == q, moved, out)
            solved[panel, :, tile * width:(tile + 1) * width] = out.astype(BF16)

    source = lax.broadcasted_iota(jnp.int32, (nrhs, width), 0)
    lane = lax.broadcasted_iota(jnp.int32, (nrhs, width), 1)
    rhs_second = contract(rhs[1], chosen(source, lane, z))
    drain(first_landed, first_recv.at[0])
    total = first_own[row]
    for slot in range(R - 1):
        total = total + first_landed[slot].astype(F32)
    first_piece[...] = total.astype(BF16)
    first_place = pl.ds(pl.multiple_of(z * bc + my_slab * slab, slab), slab)
    for which, peer in enumerate([*row_peers, row]):
        for side in range(2):
            block = my_set + side * sets
            target = panels.at[0, first_place, :]
            if which < R - 1:
                send(first_piece.at[side], target, first_send.at[1], first_recv.at[1], (peer, x * Z + block))
            else:
                @pl.when(block != z)
                def _():
                    send(first_piece.at[side], target, first_send.at[1], first_recv.at[1], (row, x * Z + block))

                @pl.when(block == z)
                def _():
                    pltpu.make_async_copy(first_piece.at[side], target, first_recv.at[1]).start()
    pass_on()
    ring_pass(1)
    drain(cross_all.at[pl.ds(0, Z - 3)], near_recv.at[1])
    cross_turned[...] = cross_all[...].reshape(Z * bc, br).T
    drain(panels.at[0], first_recv.at[1])

    crossed = contract(cross_turned[...], panels[0])
    cross_sent[...] = crossed.astype(BF16)
    for d in x_steps:
        send(cross_sent, cross_landed.at[d - 1], last_send.at[0], last_recv.at[0],
             (row, x_peer(d) * Z + z))
    first_rows[row] = first_piece[...]
    for peer in row_peers:
        send(first_piece, first_rows.at[row], first_send.at[2], first_recv.at[2], (peer, col))
    ring_pass(2, (0,))
    drain(diag_all.at[pl.ds(0, Z - 3)], near_recv.at[2])
    drain(cross_landed, last_recv.at[0])
    for d in range(X - 1):
        crossed = crossed + cross_landed[d].astype(F32)
    reduced = (rhs_second - crossed).astype(BF16)

    scatter(1, reduced)
    ring_pass(2, (1,))
    for step in range(3, half):
        ring_pass(step)
    gather(1)
    ring_wait(half, 0, 0)
    update[...] = contract_rows(panels[0], trail_all[0].reshape(Z * bc, rows))
    gathered(1)
    spread_rows(1)

    ring_wait(half, 1, 1)
    parts = 2
    part = rows // parts
    for index in range(parts):
        lanes = pl.ds(index * part, part)
        total = update[:, lanes] + contract_rows(panels[1], trail_all[1, :, :, lanes].reshape(Z * bc, part))
        update[:, lanes] = total
        update_sent[index] = total.astype(BF16).reshape(X, share, part)
        for slot, d in enumerate(x_steps):
            send(update_sent.at[index, x_peer(d)], update_landed.at[index, slot], last_send.at[1 + index],
                 last_recv.at[1 + index], (row, x_peer(d) * Z + z))
    drain(first_rows.at[pl.ds(0, R - 1)], first_recv.at[2])
    write_rows(0, [
        jnp.concatenate([first_rows[index * sets + block % sets, block // sets].astype(F32) for index in range(slabs)], axis=0)
        for block in range(Z)
    ])
    for index in range(parts):
        lanes = pl.ds(index * part, part)
        total = update[pl.ds(pl.multiple_of(x * share, share), share), lanes]
        drain(update_landed.at[index], last_recv.at[1 + index])
        for slot in range(X - 1):
            total = total + update_landed[index, slot].astype(F32)
        new[:, lanes] = old[:, lanes] - total
    drain(rows_landed.at[pl.ds(0, Z - 1)], rows_recv.at[0])
    write_rows(1, [rows_landed[block].astype(F32) for block in range(Z)])

    drain(first_landed, first_send.at[0])
    drain(panels.at[0, pl.ds(0, (R - 1) * 2 * slab), :], first_send.at[1])
    for side in range(2):
        @pl.when(my_set + side * sets != z)
        def _():
            drain(first_piece.at[side], first_send.at[1])
    drain(first_rows.at[pl.ds(0, R - 1)], first_send.at[2])
    for buffer in (cross_all, diag_all):
        drain(buffer.at[pl.ds(0, Z - 1)], near_send.at[0])
    ring_drain()
    drain(landed, sum_send.at[0])
    drain(panels.at[1, pl.ds(0, (R - 1) * piece), :], sum_send.at[1])
    drain(rows_landed.at[pl.ds(0, Z - 1)], rows_send.at[0])
    drain(cross_landed, last_send.at[0])
    for index in range(parts):
        drain(update_landed.at[index], last_send.at[1 + index])


def build(mesh, X, Z):
    R = mesh.shape["row"]

    def per_device(panel_rhs, diag_inverse, cross_block, trail_factor, trail_rhs):
        _, br, nrhs = panel_rhs.shape
        bc = diag_inverse.shape[1]
        rows = trail_factor.shape[0]
        share = nrhs // (X * Z)
        width = share * X
        piece = Z * bc // R
        slab = bc // (R // (Z // 2))
        vmem = pl.BlockSpec(memory_space=pltpu.VMEM)
        solved, new = pl.pallas_call(
            functools.partial(kernel, R, X, Z),
            out_shape=(
                pltpu.VMEM((2, bc, nrhs), BF16),
                pltpu.VMEM((share, rows), F32),
            ),
            in_specs=[pl.BlockSpec(memory_space=pltpu.HBM)] * 5,
            out_specs=(vmem, vmem),
            scratch_shapes=[
                pltpu.VMEM((2, br, nrhs), BF16),
                pltpu.VMEM((share, rows), F32),
                pltpu.VMEM((2, Z, bc, rows), BF16),
                pltpu.VMEM((bc, br), BF16),
                pltpu.VMEM((Z, bc, br), BF16),
                pltpu.VMEM((Z, bc, br), BF16),
                pltpu.VMEM((Z * bc, width), F32),
                pltpu.VMEM((R, piece, width), BF16),
                pltpu.VMEM((R - 1, piece, width), BF16),
                pltpu.VMEM((2, Z * bc, width), BF16),
                pltpu.VMEM((br, width), BF16),
                pltpu.VMEM((X - 1, br, width), BF16),
                pltpu.VMEM((width, rows), F32),
                pltpu.VMEM((2, X, share, rows // 2), BF16),
                pltpu.VMEM((2, X - 1, share, rows // 2), BF16),
                pltpu.VMEM((Z, bc, width), BF16),
                pltpu.VMEM((br, Z * bc), BF16),
                pltpu.VMEM((R, 2, slab, width), BF16),
                pltpu.VMEM((R - 1, 2, slab, width), BF16),
                pltpu.VMEM((R, 2, slab, width), F32),
                pltpu.VMEM((2, slab, width), BF16),
                pltpu.VMEM((R, 2, slab, width), BF16),
                pltpu.SemaphoreType.DMA((6,)),
                pltpu.SemaphoreType.DMA((1,)),
                pltpu.SemaphoreType.DMA((3,)),
                pltpu.SemaphoreType.DMA((2, 2, Z // 2)),
                pltpu.SemaphoreType.DMA((2, 2, Z // 2)),
                pltpu.SemaphoreType.DMA((2,)),
                pltpu.SemaphoreType.DMA((2,)),
                pltpu.SemaphoreType.DMA((1,)),
                pltpu.SemaphoreType.DMA((1,)),
                pltpu.SemaphoreType.DMA((3,)),
                pltpu.SemaphoreType.DMA((3,)),
                pltpu.SemaphoreType.DMA((3,)),
                pltpu.SemaphoreType.DMA((3,)),
            ],
            compiler_params=pltpu.CompilerParams(
                collective_id=0, has_side_effects=True, vmem_limit_bytes=63 * 1024 * 1024
            ),
        )(
            panel_rhs,
            diag_inverse,
            cross_block.T,
            jnp.transpose(trail_factor, (1, 2, 0)),
            trail_rhs.T,
        )
        return solved, new.T

    in_specs = (
        P(None, "row", None),
        P(None, "col", "row"),
        P("row", "col"),
        P("row", None, "col"),
        P("row", "col"),
    )
    out_specs = (P(None, "col", None), P("row", "col"))
    return jax.shard_map(
        per_device, mesh=mesh, in_specs=in_specs, out_specs=out_specs, check_vma=False
    )


def solution(mesh):
    return build(mesh, 4, 8)
```

```python
import functools

import jax
import jax.numpy as jnp
from jax import lax
from jax.experimental import pallas as pl
from jax.experimental.pallas import tpu as pltpu
from jax.sharding import PartitionSpec as P

MESH = pl.DeviceIdType.MESH
BF16 = jnp.bfloat16
F32 = jnp.float32


def contract_rows(left, right):
    return lax.dot_general(left, right, (((0,), (0,)), ((), ())), preferred_element_type=F32)


def contract(left, right):
    return jnp.dot(left, right, preferred_element_type=F32)


def kernel(
    R, X, Z,
    rhs_hbm, diag_hbm, cross_hbm, trail_hbm, old_hbm,
    solved, new,
    rhs, old, trail_all, diag_first, diag_all, cross_all, partial, sent, landed, panels, cross_sent, cross_landed,
    update, update_sent, update_landed, rows_landed, cross_turned, first_sent, first_landed, first_own, first_piece, first_rows,
    local_sem, near_send, near_recv, trail_send, trail_recv, sum_send, sum_recv,
    rows_send, rows_recv, last_send, last_recv, first_send, first_recv,
):
    row, col = lax.axis_index("row"), lax.axis_index("col")
    x, z = col // Z, lax.rem(col, Z)
    bc, br = diag_hbm.shape[1:]
    nrhs = rhs_hbm.shape[2]
    rows = trail_hbm.shape[2]
    share = nrhs // (X * Z)
    width = share * X
    piece = Z * bc // R

    rings = R // 2
    y, core = row // 2, lax.rem(row, 2)
    row_steps = [
        (dy, dc)
        for dy in sorted(range(rings), key=lambda d: -min(d, rings - d))
        for dc in range(2)
        if dy or dc
    ]
    row_peers = [lax.rem(y + dy, rings) * 2 + lax.rem(core + dc, 2) for dy, dc in row_steps]
    x_steps = sorted(range(1, X), key=lambda d: -min(d, X - d))
    order = sorted(range(1, Z), key=lambda d: -min(d, Z - d))

    def x_peer(d):
        return lax.rem(x + d, X)

    def z_peer(d):
        return lax.rem(z + d + Z, Z)

    sets = Z // 2
    slabs = R // sets
    slab = bc // slabs
    my_set, my_slab = lax.rem(row, sets), row // sets
    first_peers = [row] + row_peers
    bits = share.bit_length() - 1

    def chosen(target, lane, block):
        group = lax.shift_right_logical(lane, bits)
        return (target == (group * Z + block) * share + (lane & (share - 1))).astype(F32).astype(BF16)

    def send(src, dst, send_sem, recv_sem, where):
        copy = pltpu.make_async_remote_copy(
            src_ref=src, dst_ref=dst, send_sem=send_sem, recv_sem=recv_sem,
            device_id=where, device_id_type=MESH,
        )
        copy.start()

    def drain(ref, sem):
        pltpu.make_async_copy(ref, ref, sem).wait()

    loads = [
        pltpu.make_async_copy(src, dst, local_sem.at[i])
        for i, (src, dst) in enumerate([
            (rhs_hbm, rhs), (diag_hbm.at[0], diag_first), (diag_hbm.at[1], diag_all.at[z]), (cross_hbm, cross_all.at[z]),
            (trail_hbm, trail_all.at[:, z]), (old_hbm, old),
        ])
    ]
    for load in loads:
        load.start()
    barrier = pltpu.get_barrier_semaphore()
    for d in order:
        for index in range(slabs):
            giver = index * sets + lax.rem(z, sets)
            pl.semaphore_signal(barrier, inc=1, device_id=(giver, x * Z + z_peer(d)), device_id_type=MESH)
    for d in order:
        pl.semaphore_signal(barrier, inc=1, device_id=(row, x * Z + z_peer(d)), device_id_type=MESH)
    for peer in row_peers:
        pl.semaphore_signal(barrier, inc=1, device_id=(peer, col), device_id_type=MESH)
    for d in x_steps:
        pl.semaphore_signal(barrier, inc=1, device_id=(row, x_peer(d) * Z + z), device_id_type=MESH)
    at_home = (my_set == lax.rem(z, sets)).astype(jnp.int32)

    loads[0].wait()
    place = lax.shift_right_logical(lax.broadcasted_iota(jnp.int32, (br, width), 1), bits)
    tiles = [rhs[0, :, tile * width:(tile + 1) * width].astype(F32) for tile in range(Z)]
    loads[1].wait()
    for block in range(Z):
        mixed = None
        for group in range(X):
            tile, q = divmod(group * Z + block, X)
            shift = (group - q) % X * share
            moved = pltpu.roll(tiles[tile], shift, 1) if shift else tiles[tile]
            mixed = moved if mixed is None else jnp.where(place == group, moved, mixed)
        product = contract(diag_first[...], mixed.astype(BF16))
        rounded = product.astype(BF16)
        for index in range(slabs):
            first_own[index * sets + block % sets, block // sets] = product[index * slab:(index + 1) * slab]
            first_sent[index * sets + block % sets, block // sets] = rounded[index * slab:(index + 1) * slab]

    pl.semaphore_wait(barrier, (R - 1) + (X - 1) + (Z - 1) + (2 - at_home) * R)

    for slot, peer in enumerate(row_peers):
        send(first_sent.at[peer], first_landed.at[slot], first_send.at[0], first_recv.at[0], (peer, col))
    for load in loads[2:]:
        load.wait()
    for d in (2, -2, 1, -1):
        for which, buffer in enumerate((cross_all, diag_all)):
            send(buffer.at[z], buffer.at[z], near_send.at[0], near_recv.at[0 if abs(d) == 2 else 1 + which],
                 (row, x * Z + z_peer(d)))

    def pass_on():
        drain(cross_all.at[pl.ds(0, 4)], near_recv.at[0])
        for which, buffer in enumerate((cross_all, diag_all)):
            for sign in (1, -1):
                block = z_peer(-2 * sign)
                part = pl.ds(0 if sign == 1 else bc // 2, bc // 2)
                send(buffer.at[block], buffer.at[block], near_send.at[0], near_recv.at[1 + which],
                     (row, x * Z + z_peer(sign)))
                send(buffer.at[block, part, :], buffer.at[block, part, :], near_send.at[0], near_recv.at[1 + which],
                     (row, x * Z + z_peer(2 * sign)))

    half = Z // 2

    def ring_has(way, panel, step):
        return step < half or (step == half and way == panel)

    def ring_send(step, panel, way):
        if ring_has(way, panel, step):
            sign = 1 - 2 * way
            block = z_peer(-sign * (step - 1))
            send(
                trail_all.at[panel, block], trail_all.at[panel, block],
                trail_send.at[way, panel, step - 1], trail_recv.at[way, panel, step - 1],
                (row, x * Z + z_peer(sign)),
            )

    def ring_wait(step, panel, way):
        if ring_has(way, panel, step):
            drain(trail_all.at[panel, 0], trail_recv.at[way, panel, step - 1])

    def ring_pass(step, which=(0, 1)):
        for panel in which:
            for way in range(2):
                ring_wait(step, panel, way)
                ring_send(step + 1, panel, way)

    def ring_drain():
        for step in range(1, half + 1):
            for panel in range(2):
                for way in range(2):
                    if ring_has(way, panel, step):
                        drain(trail_all.at[panel, 0], trail_send.at[way, panel, step - 1])

    for panel in range(2):
        for way in range(2):
            ring_send(1, panel, way)

    def scatter(panel, right_side):
        total = contract(diag_all[...].reshape(Z * bc, br), right_side)
        partial[...] = total
        sent[...] = total.astype(BF16).reshape(R, piece, width)
        for slot, peer in enumerate(row_peers):
            send(sent.at[peer], landed.at[slot], sum_send.at[0],
                 sum_recv.at[0], (peer, col))

    def gather(panel):
        drain(landed, sum_recv.at[0])
        mine = pl.ds(pl.multiple_of(row * piece, piece), piece)
        total = partial[mine, :]
        for d in range(R - 1):
            total = total + landed[d].astype(F32)
        panels[panel, mine, :] = total.astype(BF16)
        for peer in row_peers:
            send(panels.at[panel, mine, :], panels.at[panel, mine, :], sum_send.at[1],
                 sum_recv.at[1], (peer, col))

    def gathered(panel):
        drain(panels.at[panel, pl.ds(0, (R - 1) * piece), :], sum_recv.at[1])

    def spread_rows(panel):
        own = panels[panel, pl.ds(pl.multiple_of(z * bc, bc), bc), :]
        rows_landed[z] = own
        for d in order:
            theirs = pl.ds(pl.multiple_of(z_peer(d) * bc, bc), bc)
            send(panels.at[panel, theirs, :], rows_landed.at[z], rows_send.at[0],
                 rows_recv.at[0], (row, x * Z + z_peer(d)))

    def write_rows(panel, blocks):
        place = lax.shift_right_logical(lax.broadcasted_iota(jnp.int32, (bc, width), 1), bits)
        for tile in range(Z):
            group, first = divmod(tile * X, Z)
            out = None
            for q in range(X):
                shift = (q - group) % X * share
                moved = pltpu.roll(blocks[first + q], shift, 1) if shift else blocks[first + q]
                out = moved if out is None else jnp.where(place == q, moved, out)
            solved[panel, :, tile * width:(tile + 1) * width] = out.astype(BF16)

    source = lax.broadcasted_iota(jnp.int32, (nrhs, width), 0)
    lane = lax.broadcasted_iota(jnp.int32, (nrhs, width), 1)
    rhs_second = contract(rhs[1], chosen(source, lane, z))
    drain(first_landed, first_recv.at[0])
    total = first_own[row]
    for slot in range(R - 1):
        total = total + first_landed[slot].astype(F32)
    first_piece[...] = total.astype(BF16)
    first_place = pl.ds(pl.multiple_of(z * bc + my_slab * slab, slab), slab)
    for which, peer in enumerate([*row_peers, row]):
        for side in range(2):
            block = my_set + side * sets
            target = panels.at[0, first_place, :]
            if which < R - 1:
                send(first_piece.at[side], target, first_send.at[1], first_recv.at[1], (peer, x * Z + block))
            else:
                @pl.when(block != z)
                def _():
                    send(first_piece.at[side], target, first_send.at[1], first_recv.at[1], (row, x * Z + block))

                @pl.when(block == z)
                def _():
                    pltpu.make_async_copy(first_piece.at[side], target, first_recv.at[1]).start()
    pass_on()
    ring_pass(1)
    drain(cross_all.at[pl.ds(0, Z - 3)], near_recv.at[1])
    cross_turned[...] = cross_all[...].reshape(Z * bc, br).T
    drain(panels.at[0], first_recv.at[1])

    crossed = contract(cross_turned[...], panels[0])
    cross_sent[...] = crossed.astype(BF16)
    for d in x_steps:
        send(cross_sent, cross_landed.at[d - 1], last_send.at[0], last_recv.at[0],
             (row, x_peer(d) * Z + z))
    first_rows[row] = first_piece[...]
    for peer in row_peers:
        send(first_piece, first_rows.at[row], first_send.at[2], first_recv.at[2], (peer, col))
    ring_pass(2, (0,))
    drain(diag_all.at[pl.ds(0, Z - 3)], near_recv.at[2])
    drain(cross_landed, last_recv.at[0])
    for d in range(X - 1):
        crossed = crossed + cross_landed[d].astype(F32)
    reduced = (rhs_second - crossed).astype(BF16)

    scatter(1, reduced)
    ring_pass(2, (1,))
    for step in range(3, half):
        ring_pass(step)
    gather(1)
    ring_wait(half, 0, 0)
    update[...] = contract_rows(panels[0], trail_all[0].reshape(Z * bc, rows))
    gathered(1)
    spread_rows(1)

    ring_wait(half, 1, 1)
    second_turned = panels[1].T
    parts = 2
    part = rows // parts
    for index in range(parts):
        lanes = pl.ds(index * part, part)
        total = update[:, lanes] + contract(second_turned, trail_all[1, :, :, lanes].reshape(Z * bc, part))
        update[:, lanes] = total
        update_sent[index] = total.astype(BF16).reshape(X, share, part)
        for slot, d in enumerate(x_steps):
            send(update_sent.at[index, x_peer(d)], update_landed.at[index, slot], last_send.at[1 + index],
                 last_recv.at[1 + index], (row, x_peer(d) * Z + z))
    drain(first_rows.at[pl.ds(0, R - 1)], first_recv.at[2])
    write_rows(0, [
        jnp.concatenate([first_rows[index * sets + block % sets, block // sets].astype(F32) for index in range(slabs)], axis=0)
        for block in range(Z)
    ])
    for index in range(parts):
        lanes = pl.ds(index * part, part)
        total = update[pl.ds(pl.multiple_of(x * share, share), share), lanes]
        drain(update_landed.at[index], last_recv.at[1 + index])
        for slot in range(X - 1):
            total = total + update_landed[index, slot].astype(F32)
        new[:, lanes] = old[:, lanes] - total
    drain(rows_landed.at[pl.ds(0, Z - 1)], rows_recv.at[0])
    write_rows(1, [rows_landed[block].astype(F32) for block in range(Z)])

    drain(first_landed, first_send.at[0])
    drain(panels.at[0, pl.ds(0, (R - 1) * 2 * slab), :], first_send.at[1])
    for side in range(2):
        @pl.when(my_set + side * sets != z)
        def _():
            drain(first_piece.at[side], first_send.at[1])
    drain(first_rows.at[pl.ds(0, R - 1)], first_send.at[2])
    for buffer in (cross_all, diag_all):
        drain(buffer.at[pl.ds(0, Z - 1)], near_send.at[0])
    ring_drain()
    drain(landed, sum_send.at[0])
    drain(panels.at[1, pl.ds(0, (R - 1) * piece), :], sum_send.at[1])
    drain(rows_landed.at[pl.ds(0, Z - 1)], rows_send.at[0])
    drain(cross_landed, last_send.at[0])
    for index in range(parts):
        drain(update_landed.at[index], last_send.at[1 + index])


def build(mesh, X, Z):
    R = mesh.shape["row"]

    def per_device(panel_rhs, diag_inverse, cross_block, trail_factor, trail_rhs):
        _, br, nrhs = panel_rhs.shape
        bc = diag_inverse.shape[1]
        rows = trail_factor.shape[0]
        share = nrhs // (X * Z)
        width = share * X
        piece = Z * bc // R
        slab = bc // (R // (Z // 2))
        vmem = pl.BlockSpec(memory_space=pltpu.VMEM)
        solved, new = pl.pallas_call(
            functools.partial(kernel, R, X, Z),
            out_shape=(
                pltpu.VMEM((2, bc, nrhs), BF16),
                pltpu.VMEM((share, rows), F32),
            ),
            in_specs=[pl.BlockSpec(memory_space=pltpu.HBM)] * 5,
            out_specs=(vmem, vmem),
            scratch_shapes=[
                pltpu.VMEM((2, br, nrhs), BF16),
                pltpu.VMEM((share, rows), F32),
                pltpu.VMEM((2, Z, bc, rows), BF16),
                pltpu.VMEM((bc, br), BF16),
                pltpu.VMEM((Z, bc, br), BF16),
                pltpu.VMEM((Z, bc, br), BF16),
                pltpu.VMEM((Z * bc, width), F32),
                pltpu.VMEM((R, piece, width), BF16),
                pltpu.VMEM((R - 1, piece, width), BF16),
                pltpu.VMEM((2, Z * bc, width), BF16),
                pltpu.VMEM((br, width), BF16),
                pltpu.VMEM((X - 1, br, width), BF16),
                pltpu.VMEM((width, rows), F32),
                pltpu.VMEM((2, X, share, rows // 2), BF16),
                pltpu.VMEM((2, X - 1, share, rows // 2), BF16),
                pltpu.VMEM((Z, bc, width), BF16),
                pltpu.VMEM((br, Z * bc), BF16),
                pltpu.VMEM((R, 2, slab, width), BF16),
                pltpu.VMEM((R - 1, 2, slab, width), BF16),
                pltpu.VMEM((R, 2, slab, width), F32),
                pltpu.VMEM((2, slab, width), BF16),
                pltpu.VMEM((R, 2, slab, width), BF16),
                pltpu.SemaphoreType.DMA((6,)),
                pltpu.SemaphoreType.DMA((1,)),
                pltpu.SemaphoreType.DMA((3,)),
                pltpu.SemaphoreType.DMA((2, 2, Z // 2)),
                pltpu.SemaphoreType.DMA((2, 2, Z // 2)),
                pltpu.SemaphoreType.DMA((2,)),
                pltpu.SemaphoreType.DMA((2,)),
                pltpu.SemaphoreType.DMA((1,)),
                pltpu.SemaphoreType.DMA((1,)),
                pltpu.SemaphoreType.DMA((3,)),
                pltpu.SemaphoreType.DMA((3,)),
                pltpu.SemaphoreType.DMA((3,)),
                pltpu.SemaphoreType.DMA((3,)),
            ],
            compiler_params=pltpu.CompilerParams(
                collective_id=0, has_side_effects=True, vmem_limit_bytes=63 * 1024 * 1024
            ),
        )(
            panel_rhs,
            diag_inverse,
            cross_block.T,
            jnp.transpose(trail_factor, (1, 2, 0)),
            trail_rhs.T,
        )
        return solved, new.T

    in_specs = (
        P(None, "row", None),
        P(None, "col", "row"),
        P("row", "col"),
        P("row", None, "col"),
        P("row", "col"),
    )
    out_specs = (P(None, "col", None), P("row", "col"))
    return jax.shard_map(
        per_device, mesh=mesh, in_specs=in_specs, out_specs=out_specs, check_vma=False
    )


def solution(mesh):
    return build(mesh, 4, 8)
```

```python
import functools

import jax
import jax.numpy as jnp
from jax import lax
from jax.experimental import pallas as pl
from jax.experimental.pallas import tpu as pltpu
from jax.sharding import PartitionSpec as P

MESH = pl.DeviceIdType.MESH
BF16 = jnp.bfloat16
F32 = jnp.float32


def contract_rows(left, right):
    return lax.dot_general(left, right, (((0,), (0,)), ((), ())), preferred_element_type=F32)


def contract(left, right):
    return jnp.dot(left, right, preferred_element_type=F32)


def kernel(
    R, X, Z,
    rhs_hbm, diag_hbm, cross_hbm, trail_hbm, old_hbm,
    solved, new,
    rhs, old, trail_all, diag_first, diag_all, cross_all, partial, sent, landed, panels, cross_sent, cross_landed,
    update, update_sent, update_landed, rows_landed, cross_turned, first_sent, first_landed, first_own, first_piece, first_rows,
    local_sem, near_send, near_recv, trail_send, trail_recv, sum_send, sum_recv,
    rows_send, rows_recv, last_send, last_recv, first_send, first_recv,
):
    row, col = lax.axis_index("row"), lax.axis_index("col")
    x, z = col // Z, lax.rem(col, Z)
    bc, br = diag_hbm.shape[1:]
    nrhs = rhs_hbm.shape[2]
    rows = trail_hbm.shape[2]
    share = nrhs // (X * Z)
    width = share * X
    piece = Z * bc // R

    rings = R // 2
    y, core = row // 2, lax.rem(row, 2)
    row_steps = [
        (dy, dc)
        for dy in sorted(range(rings), key=lambda d: -min(d, rings - d))
        for dc in range(2)
        if dy or dc
    ]
    row_peers = [lax.rem(y + dy, rings) * 2 + lax.rem(core + dc, 2) for dy, dc in row_steps]
    x_steps = sorted(range(1, X), key=lambda d: -min(d, X - d))
    order = sorted(range(1, Z), key=lambda d: -min(d, Z - d))

    def x_peer(d):
        return lax.rem(x + d, X)

    def z_peer(d):
        return lax.rem(z + d + Z, Z)

    sets = Z // 2
    slabs = R // sets
    slab = bc // slabs
    my_set, my_slab = lax.rem(row, sets), row // sets
    first_peers = [row] + row_peers
    bits = share.bit_length() - 1

    def chosen(target, lane, block):
        group = lax.shift_right_logical(lane, bits)
        return (target == (group * Z + block) * share + (lane & (share - 1))).astype(F32).astype(BF16)

    def send(src, dst, send_sem, recv_sem, where):
        copy = pltpu.make_async_remote_copy(
            src_ref=src, dst_ref=dst, send_sem=send_sem, recv_sem=recv_sem,
            device_id=where, device_id_type=MESH,
        )
        copy.start()

    def drain(ref, sem):
        pltpu.make_async_copy(ref, ref, sem).wait()

    loads = [
        pltpu.make_async_copy(src, dst, local_sem.at[i])
        for i, (src, dst) in enumerate([
            (rhs_hbm, rhs), (diag_hbm.at[0], diag_first), (diag_hbm.at[1], diag_all.at[z]), (cross_hbm, cross_all.at[z]),
            (trail_hbm, trail_all.at[:, z]), (old_hbm, old),
        ])
    ]
    for load in loads:
        load.start()
    barrier = pltpu.get_barrier_semaphore()
    for d in order:
        for index in range(slabs):
            giver = index * sets + lax.rem(z, sets)
            pl.semaphore_signal(barrier, inc=1, device_id=(giver, x * Z + z_peer(d)), device_id_type=MESH)
    for d in order:
        pl.semaphore_signal(barrier, inc=1, device_id=(row, x * Z + z_peer(d)), device_id_type=MESH)
    for peer in row_peers:
        pl.semaphore_signal(barrier, inc=1, device_id=(peer, col), device_id_type=MESH)
    for d in x_steps:
        pl.semaphore_signal(barrier, inc=1, device_id=(row, x_peer(d) * Z + z), device_id_type=MESH)
    at_home = (my_set == lax.rem(z, sets)).astype(jnp.int32)

    loads[0].wait()
    place = lax.shift_right_logical(lax.broadcasted_iota(jnp.int32, (br, width), 1), bits)
    tiles = [rhs[0, :, tile * width:(tile + 1) * width].astype(F32) for tile in range(Z)]
    loads[1].wait()
    for block in range(Z):
        mixed = None
        for group in range(X):
            tile, q = divmod(group * Z + block, X)
            shift = (group - q) % X * share
            moved = pltpu.roll(tiles[tile], shift, 1) if shift else tiles[tile]
            mixed = moved if mixed is None else jnp.where(place == group, moved, mixed)
        product = contract(diag_first[...], mixed.astype(BF16))
        rounded = product.astype(BF16)
        for index in range(slabs):
            first_own[index * sets + block % sets, block // sets] = product[index * slab:(index + 1) * slab]
            first_sent[index * sets + block % sets, block // sets] = rounded[index * slab:(index + 1) * slab]

    pl.semaphore_wait(barrier, (R - 1) + (X - 1) + (Z - 1) + (2 - at_home) * R)

    for slot, peer in enumerate(row_peers):
        send(first_sent.at[peer], first_landed.at[slot], first_send.at[0], first_recv.at[0], (peer, col))
    for load in loads[2:]:
        load.wait()
    for which, buffer in enumerate((cross_all, diag_all)):
        for d in (2, -2, 1, -1):
            send(buffer.at[z], buffer.at[z], near_send.at[0], near_recv.at[which + (2 if abs(d) == 2 else 0)],
                 (row, x * Z + z_peer(d)))

    def pass_on(which, buffer):
        drain(buffer.at[pl.ds(0, 2)], near_recv.at[which + 2])
        for sign in (1, -1):
            block = z_peer(-2 * sign)
            part = pl.ds(0 if sign == 1 else bc // 2, bc // 2)
            send(buffer.at[block], buffer.at[block], near_send.at[0], near_recv.at[which],
                 (row, x * Z + z_peer(sign)))
            send(buffer.at[block, part, :], buffer.at[block, part, :], near_send.at[0], near_recv.at[which],
                 (row, x * Z + z_peer(2 * sign)))

    half = Z // 2

    def ring_has(way, panel, step):
        return step < half or (step == half and way == panel)

    def ring_send(step, panel, way):
        if ring_has(way, panel, step):
            sign = 1 - 2 * way
            block = z_peer(-sign * (step - 1))
            send(
                trail_all.at[panel, block], trail_all.at[panel, block],
                trail_send.at[way, panel, step - 1], trail_recv.at[way, panel, step - 1],
                (row, x * Z + z_peer(sign)),
            )

    def ring_wait(step, panel, way):
        if ring_has(way, panel, step):
            drain(trail_all.at[panel, 0], trail_recv.at[way, panel, step - 1])

    def ring_pass(step, which=(0, 1)):
        for panel in which:
            for way in range(2):
                ring_wait(step, panel, way)
                ring_send(step + 1, panel, way)

    def ring_drain():
        for step in range(1, half + 1):
            for panel in range(2):
                for way in range(2):
                    if ring_has(way, panel, step):
                        drain(trail_all.at[panel, 0], trail_send.at[way, panel, step - 1])

    for panel in range(2):
        for way in range(2):
            ring_send(1, panel, way)

    def scatter(panel, right_side):
        total = contract(diag_all[...].reshape(Z * bc, br), right_side)
        partial[...] = total
        sent[...] = total.astype(BF16).reshape(R, piece, width)
        for slot, peer in enumerate(row_peers):
            send(sent.at[peer], landed.at[slot], sum_send.at[0],
                 sum_recv.at[0], (peer, col))

    def gather(panel):
        drain(landed, sum_recv.at[0])
        mine = pl.ds(pl.multiple_of(row * piece, piece), piece)
        total = partial[mine, :]
        for d in range(R - 1):
            total = total + landed[d].astype(F32)
        panels[panel, mine, :] = total.astype(BF16)
        for peer in row_peers:
            send(panels.at[panel, mine, :], panels.at[panel, mine, :], sum_send.at[1],
                 sum_recv.at[1], (peer, col))

    def gathered(panel):
        drain(panels.at[panel, pl.ds(0, (R - 1) * piece), :], sum_recv.at[1])

    def spread_rows(panel):
        own = panels[panel, pl.ds(pl.multiple_of(z * bc, bc), bc), :]
        rows_landed[z] = own
        for d in order:
            theirs = pl.ds(pl.multiple_of(z_peer(d) * bc, bc), bc)
            send(panels.at[panel, theirs, :], rows_landed.at[z], rows_send.at[0],
                 rows_recv.at[0], (row, x * Z + z_peer(d)))

    def write_rows(panel, blocks):
        place = lax.shift_right_logical(lax.broadcasted_iota(jnp.int32, (bc, width), 1), bits)
        for tile in range(Z):
            group, first = divmod(tile * X, Z)
            out = None
            for q in range(X):
                shift = (q - group) % X * share
                moved = pltpu.roll(blocks[first + q], shift, 1) if shift else blocks[first + q]
                out = moved if out is None else jnp.where(place == q, moved, out)
            solved[panel, :, tile * width:(tile + 1) * width] = out.astype(BF16)

    source = lax.broadcasted_iota(jnp.int32, (nrhs, width), 0)
    lane = lax.broadcasted_iota(jnp.int32, (nrhs, width), 1)
    rhs_second = contract(rhs[1], chosen(source, lane, z))
    pass_on(0, cross_all)
    drain(first_landed, first_recv.at[0])
    total = first_own[row]
    for slot in range(R - 1):
        total = total + first_landed[slot].astype(F32)
    first_piece[...] = total.astype(BF16)
    first_place = pl.ds(pl.multiple_of(z * bc + my_slab * slab, slab), slab)
    for which, peer in enumerate([*row_peers, row]):
        for side in range(2):
            block = my_set + side * sets
            target = panels.at[0, first_place, :]
            if which < R - 1:
                send(first_piece.at[side], target, first_send.at[1], first_recv.at[1], (peer, x * Z + block))
            else:
                @pl.when(block != z)
                def _():
                    send(first_piece.at[side], target, first_send.at[1], first_recv.at[1], (row, x * Z + block))

                @pl.when(block == z)
                def _():
                    pltpu.make_async_copy(first_piece.at[side], target, first_recv.at[1]).start()
    pass_on(1, diag_all)
    ring_pass(1)
    drain(cross_all.at[pl.ds(0, Z - 3)], near_recv.at[0])
    cross_turned[...] = cross_all[...].reshape(Z * bc, br).T
    drain(panels.at[0], first_recv.at[1])

    crossed = contract(cross_turned[...], panels[0])
    cross_sent[...] = crossed.astype(BF16)
    for d in x_steps:
        send(cross_sent, cross_landed.at[d - 1], last_send.at[0], last_recv.at[0],
             (row, x_peer(d) * Z + z))
    first_rows[row] = first_piece[...]
    for peer in row_peers:
        send(first_piece, first_rows.at[row], first_send.at[2], first_recv.at[2], (peer, col))
    ring_pass(2, (0,))
    drain(diag_all.at[pl.ds(0, Z - 3)], near_recv.at[1])
    drain(cross_landed, last_recv.at[0])
    for d in range(X - 1):
        crossed = crossed + cross_landed[d].astype(F32)
    reduced = (rhs_second - crossed).astype(BF16)

    scatter(1, reduced)
    ring_pass(2, (1,))
    for step in range(3, half):
        ring_pass(step)
    gather(1)
    ring_wait(half, 0, 0)
    update[...] = contract_rows(panels[0], trail_all[0].reshape(Z * bc, rows))
    gathered(1)
    spread_rows(1)

    ring_wait(half, 1, 1)
    second_turned = panels[1].T
    parts = 2
    part = rows // parts
    for index in range(parts):
        lanes = pl.ds(index * part, part)
        total = update[:, lanes] + contract(second_turned, trail_all[1, :, :, lanes].reshape(Z * bc, part))
        update[:, lanes] = total
        update_sent[index] = total.astype(BF16).reshape(X, share, part)
        for slot, d in enumerate(x_steps):
            send(update_sent.at[index, x_peer(d)], update_landed.at[index, slot], last_send.at[1 + index],
                 last_recv.at[1 + index], (row, x_peer(d) * Z + z))
    drain(first_rows.at[pl.ds(0, R - 1)], first_recv.at[2])
    write_rows(0, [
        jnp.concatenate([first_rows[index * sets + block % sets, block // sets].astype(F32) for index in range(slabs)], axis=0)
        for block in range(Z)
    ])
    for index in range(parts):
        lanes = pl.ds(index * part, part)
        total = update[pl.ds(pl.multiple_of(x * share, share), share), lanes]
        drain(update_landed.at[index], last_recv.at[1 + index])
        for slot in range(X - 1):
            total = total + update_landed[index, slot].astype(F32)
        new[:, lanes] = old[:, lanes] - total
    drain(rows_landed.at[pl.ds(0, Z - 1)], rows_recv.at[0])
    write_rows(1, [rows_landed[block].astype(F32) for block in range(Z)])

    drain(first_landed, first_send.at[0])
    drain(panels.at[0, pl.ds(0, (R - 1) * 2 * slab), :], first_send.at[1])
    for side in range(2):
        @pl.when(my_set + side * sets != z)
        def _():
            drain(first_piece.at[side], first_send.at[1])
    drain(first_rows.at[pl.ds(0, R - 1)], first_send.at[2])
    for buffer in (cross_all, diag_all):
        drain(buffer.at[pl.ds(0, Z - 1)], near_send.at[0])
    ring_drain()
    drain(landed, sum_send.at[0])
    drain(panels.at[1, pl.ds(0, (R - 1) * piece), :], sum_send.at[1])
    drain(rows_landed.at[pl.ds(0, Z - 1)], rows_send.at[0])
    drain(cross_landed, last_send.at[0])
    for index in range(parts):
        drain(update_landed.at[index], last_send.at[1 + index])


def build(mesh, X, Z):
    R = mesh.shape["row"]

    def per_device(panel_rhs, diag_inverse, cross_block, trail_factor, trail_rhs):
        _, br, nrhs = panel_rhs.shape
        bc = diag_inverse.shape[1]
        rows = trail_factor.shape[0]
        share = nrhs // (X * Z)
        width = share * X
        piece = Z * bc // R
        slab = bc // (R // (Z // 2))
        vmem = pl.BlockSpec(memory_space=pltpu.VMEM)
        solved, new = pl.pallas_call(
            functools.partial(kernel, R, X, Z),
            out_shape=(
                pltpu.VMEM((2, bc, nrhs), BF16),
                pltpu.VMEM((share, rows), F32),
            ),
            in_specs=[pl.BlockSpec(memory_space=pltpu.HBM)] * 5,
            out_specs=(vmem, vmem),
            scratch_shapes=[
                pltpu.VMEM((2, br, nrhs), BF16),
                pltpu.VMEM((share, rows), F32),
                pltpu.VMEM((2, Z, bc, rows), BF16),
                pltpu.VMEM((bc, br), BF16),
                pltpu.VMEM((Z, bc, br), BF16),
                pltpu.VMEM((Z, bc, br), BF16),
                pltpu.VMEM((Z * bc, width), F32),
                pltpu.VMEM((R, piece, width), BF16),
                pltpu.VMEM((R - 1, piece, width), BF16),
                pltpu.VMEM((2, Z * bc, width), BF16),
                pltpu.VMEM((br, width), BF16),
                pltpu.VMEM((X - 1, br, width), BF16),
                pltpu.VMEM((width, rows), F32),
                pltpu.VMEM((2, X, share, rows // 2), BF16),
                pltpu.VMEM((2, X - 1, share, rows // 2), BF16),
                pltpu.VMEM((Z, bc, width), BF16),
                pltpu.VMEM((br, Z * bc), BF16),
                pltpu.VMEM((R, 2, slab, width), BF16),
                pltpu.VMEM((R - 1, 2, slab, width), BF16),
                pltpu.VMEM((R, 2, slab, width), F32),
                pltpu.VMEM((2, slab, width), BF16),
                pltpu.VMEM((R, 2, slab, width), BF16),
                pltpu.SemaphoreType.DMA((6,)),
                pltpu.SemaphoreType.DMA((1,)),
                pltpu.SemaphoreType.DMA((4,)),
                pltpu.SemaphoreType.DMA((2, 2, Z // 2)),
                pltpu.SemaphoreType.DMA((2, 2, Z // 2)),
                pltpu.SemaphoreType.DMA((2,)),
                pltpu.SemaphoreType.DMA((2,)),
                pltpu.SemaphoreType.DMA((1,)),
                pltpu.SemaphoreType.DMA((1,)),
                pltpu.SemaphoreType.DMA((3,)),
                pltpu.SemaphoreType.DMA((3,)),
                pltpu.SemaphoreType.DMA((3,)),
                pltpu.SemaphoreType.DMA((3,)),
            ],
            compiler_params=pltpu.CompilerParams(
                collective_id=0, has_side_effects=True, vmem_limit_bytes=63 * 1024 * 1024
            ),
        )(
            panel_rhs,
            diag_inverse,
            cross_block.T,
            jnp.transpose(trail_factor, (1, 2, 0)),
            trail_rhs.T,
        )
        return solved, new.T

    in_specs = (
        P(None, "row", None),
        P(None, "col", "row"),
        P("row", "col"),
        P("row", None, "col"),
        P("row", "col"),
    )
    out_specs = (P(None, "col", None), P("row", "col"))
    return jax.shard_map(
        per_device, mesh=mesh, in_specs=in_specs, out_specs=out_specs, check_vma=False
    )


def solution(mesh):
    return build(mesh, 4, 8)
```

```python
import functools

import jax
import jax.numpy as jnp
from jax import lax
from jax.experimental import pallas as pl
from jax.experimental.pallas import tpu as pltpu
from jax.sharding import PartitionSpec as P

MESH = pl.DeviceIdType.MESH
BF16 = jnp.bfloat16
F32 = jnp.float32


def contract_rows(left, right):
    return lax.dot_general(left, right, (((0,), (0,)), ((), ())), preferred_element_type=F32)


def contract(left, right):
    return jnp.dot(left, right, preferred_element_type=F32)


def kernel(
    R, X, Z,
    rhs_hbm, diag_hbm, cross_hbm, trail_hbm, old_hbm,
    solved, new,
    rhs, old, trail_all, diag_first, diag_all, cross_all, partial, sent, landed, panels, cross_sent, cross_landed,
    update, update_sent, update_landed, rows_landed, cross_turned, first_sent, first_landed, first_own, first_piece, first_rows,
    local_sem, near_send, near_recv, trail_send, trail_recv, sum_send, sum_recv,
    rows_send, rows_recv, last_send, last_recv, first_send, first_recv,
):
    row, col = lax.axis_index("row"), lax.axis_index("col")
    x, z = col // Z, lax.rem(col, Z)
    bc, br = diag_hbm.shape[1:]
    nrhs = rhs_hbm.shape[2]
    rows = trail_hbm.shape[2]
    share = nrhs // (X * Z)
    width = share * X
    piece = Z * bc // R

    rings = R // 2
    y, core = row // 2, lax.rem(row, 2)
    row_steps = [
        (dy, dc)
        for dy in sorted(range(rings), key=lambda d: -min(d, rings - d))
        for dc in range(2)
        if dy or dc
    ]
    row_peers = [lax.rem(y + dy, rings) * 2 + lax.rem(core + dc, 2) for dy, dc in row_steps]
    x_steps = sorted(range(1, X), key=lambda d: -min(d, X - d))
    order = sorted(range(1, Z), key=lambda d: -min(d, Z - d))

    def x_peer(d):
        return lax.rem(x + d, X)

    def z_peer(d):
        return lax.rem(z + d + Z, Z)

    sets = Z // 2
    slabs = R // sets
    slab = bc // slabs
    my_set, my_slab = lax.rem(row, sets), row // sets
    first_peers = [row] + row_peers
    bits = share.bit_length() - 1

    def chosen(target, lane, block):
        group = lax.shift_right_logical(lane, bits)
        return (target == (group * Z + block) * share + (lane & (share - 1))).astype(F32).astype(BF16)

    def send(src, dst, send_sem, recv_sem, where):
        copy = pltpu.make_async_remote_copy(
            src_ref=src, dst_ref=dst, send_sem=send_sem, recv_sem=recv_sem,
            device_id=where, device_id_type=MESH,
        )
        copy.start()

    def drain(ref, sem):
        pltpu.make_async_copy(ref, ref, sem).wait()

    loads = [
        pltpu.make_async_copy(src, dst, local_sem.at[i])
        for i, (src, dst) in enumerate([
            (rhs_hbm, rhs), (diag_hbm.at[0], diag_first), (diag_hbm.at[1], diag_all.at[z]), (cross_hbm, cross_all.at[z]),
            (trail_hbm, trail_all.at[:, z]), (old_hbm, old),
        ])
    ]
    for load in loads:
        load.start()
    barrier = pltpu.get_barrier_semaphore()
    for d in order:
        for index in range(slabs):
            giver = index * sets + lax.rem(z, sets)
            pl.semaphore_signal(barrier, inc=1, device_id=(giver, x * Z + z_peer(d)), device_id_type=MESH)
    for d in order:
        pl.semaphore_signal(barrier, inc=1, device_id=(row, x * Z + z_peer(d)), device_id_type=MESH)
    for peer in row_peers:
        pl.semaphore_signal(barrier, inc=1, device_id=(peer, col), device_id_type=MESH)
    for d in x_steps:
        pl.semaphore_signal(barrier, inc=1, device_id=(row, x_peer(d) * Z + z), device_id_type=MESH)
    at_home = (my_set == lax.rem(z, sets)).astype(jnp.int32)

    loads[0].wait()
    place = lax.shift_right_logical(lax.broadcasted_iota(jnp.int32, (br, width), 1), bits)
    tiles = [rhs[0, :, tile * width:(tile + 1) * width].astype(F32) for tile in range(Z)]
    loads[1].wait()
    for block in range(Z):
        mixed = None
        for group in range(X):
            tile, q = divmod(group * Z + block, X)
            shift = (group - q) % X * share
            moved = pltpu.roll(tiles[tile], shift, 1) if shift else tiles[tile]
            mixed = moved if mixed is None else jnp.where(place == group, moved, mixed)
        product = contract(diag_first[...], mixed.astype(BF16))
        rounded = product.astype(BF16)
        for index in range(slabs):
            first_own[index * sets + block % sets, block // sets] = product[index * slab:(index + 1) * slab]
            first_sent[index * sets + block % sets, block // sets] = rounded[index * slab:(index + 1) * slab]

    pl.semaphore_wait(barrier, (R - 1) + (X - 1) + (Z - 1) + (2 - at_home) * R)

    for load in loads[2:]:
        load.wait()
    for d in (2, -2, 1, -1):
        for which, buffer in enumerate((cross_all, diag_all)):
            send(buffer.at[z], buffer.at[z], near_send.at[0], near_recv.at[0 if abs(d) == 2 else 1 + which],
                 (row, x * Z + z_peer(d)))

    for slot, peer in enumerate(row_peers):
        send(first_sent.at[peer], first_landed.at[slot], first_send.at[0], first_recv.at[0], (peer, col))

    def pass_on():
        drain(cross_all.at[pl.ds(0, 4)], near_recv.at[0])
        for which, buffer in enumerate((cross_all, diag_all)):
            for sign in (1, -1):
                block = z_peer(-2 * sign)
                part = pl.ds(0 if sign == 1 else bc // 2, bc // 2)
                send(buffer.at[block], buffer.at[block], near_send.at[0], near_recv.at[1 + which],
                     (row, x * Z + z_peer(sign)))
                send(buffer.at[block, part, :], buffer.at[block, part, :], near_send.at[0], near_recv.at[1 + which],
                     (row, x * Z + z_peer(2 * sign)))

    half = Z // 2

    def ring_has(way, panel, step):
        return step < half or (step == half and way == panel)

    def ring_send(step, panel, way):
        if ring_has(way, panel, step):
            sign = 1 - 2 * way
            block = z_peer(-sign * (step - 1))
            send(
                trail_all.at[panel, block], trail_all.at[panel, block],
                trail_send.at[way, panel, step - 1], trail_recv.at[way, panel, step - 1],
                (row, x * Z + z_peer(sign)),
            )

    def ring_wait(step, panel, way):
        if ring_has(way, panel, step):
            drain(trail_all.at[panel, 0], trail_recv.at[way, panel, step - 1])

    def ring_pass(step, which=(0, 1)):
        for panel in which:
            for way in range(2):
                ring_wait(step, panel, way)
                ring_send(step + 1, panel, way)

    def ring_drain():
        for step in range(1, half + 1):
            for panel in range(2):
                for way in range(2):
                    if ring_has(way, panel, step):
                        drain(trail_all.at[panel, 0], trail_send.at[way, panel, step - 1])

    for panel in range(2):
        for way in range(2):
            ring_send(1, panel, way)

    def scatter(panel, right_side):
        total = contract(diag_all[...].reshape(Z * bc, br), right_side)
        partial[...] = total
        sent[...] = total.astype(BF16).reshape(R, piece, width)
        for slot, peer in enumerate(row_peers):
            send(sent.at[peer], landed.at[slot], sum_send.at[0],
                 sum_recv.at[0], (peer, col))

    def gather(panel):
        drain(landed, sum_recv.at[0])
        mine = pl.ds(pl.multiple_of(row * piece, piece), piece)
        total = partial[mine, :]
        for d in range(R - 1):
            total = total + landed[d].astype(F32)
        panels[panel, mine, :] = total.astype(BF16)
        for peer in row_peers:
            send(panels.at[panel, mine, :], panels.at[panel, mine, :], sum_send.at[1],
                 sum_recv.at[1], (peer, col))

    def gathered(panel):
        drain(panels.at[panel, pl.ds(0, (R - 1) * piece), :], sum_recv.at[1])

    def spread_rows(panel):
        own = panels[panel, pl.ds(pl.multiple_of(z * bc, bc), bc), :]
        rows_landed[z] = own
        for d in order:
            theirs = pl.ds(pl.multiple_of(z_peer(d) * bc, bc), bc)
            send(panels.at[panel, theirs, :], rows_landed.at[z], rows_send.at[0],
                 rows_recv.at[0], (row, x * Z + z_peer(d)))

    def write_rows(panel, blocks):
        place = lax.shift_right_logical(lax.broadcasted_iota(jnp.int32, (bc, width), 1), bits)
        for tile in range(Z):
            group, first = divmod(tile * X, Z)
            out = None
            for q in range(X):
                shift = (q - group) % X * share
                moved = pltpu.roll(blocks[first + q], shift, 1) if shift else blocks[first + q]
                out = moved if out is None else jnp.where(place == q, moved, out)
            solved[panel, :, tile * width:(tile + 1) * width] = out.astype(BF16)

    source = lax.broadcasted_iota(jnp.int32, (nrhs, width), 0)
    lane = lax.broadcasted_iota(jnp.int32, (nrhs, width), 1)
    rhs_second = contract(rhs[1], chosen(source, lane, z))
    drain(first_landed, first_recv.at[0])
    total = first_own[row]
    for slot in range(R - 1):
        total = total + first_landed[slot].astype(F32)
    first_piece[...] = total.astype(BF16)
    first_place = pl.ds(pl.multiple_of(z * bc + my_slab * slab, slab), slab)
    for which, peer in enumerate([*row_peers, row]):
        for side in range(2):
            block = my_set + side * sets
            target = panels.at[0, first_place, :]
            if which < R - 1:
                send(first_piece.at[side], target, first_send.at[1], first_recv.at[1], (peer, x * Z + block))
            else:
                @pl.when(block != z)
                def _():
                    send(first_piece.at[side], target, first_send.at[1], first_recv.at[1], (row, x * Z + block))

                @pl.when(block == z)
                def _():
                    pltpu.make_async_copy(first_piece.at[side], target, first_recv.at[1]).start()
    pass_on()
    ring_pass(1)
    drain(cross_all.at[pl.ds(0, Z - 3)], near_recv.at[1])
    cross_turned[...] = cross_all[...].reshape(Z * bc, br).T
    drain(panels.at[0], first_recv.at[1])

    crossed = contract(cross_turned[...], panels[0])
    cross_sent[...] = crossed.astype(BF16)
    for d in x_steps:
        send(cross_sent, cross_landed.at[d - 1], last_send.at[0], last_recv.at[0],
             (row, x_peer(d) * Z + z))
    first_rows[row] = first_piece[...]
    for peer in row_peers:
        send(first_piece, first_rows.at[row], first_send.at[2], first_recv.at[2], (peer, col))
    ring_pass(2, (0,))
    drain(diag_all.at[pl.ds(0, Z - 3)], near_recv.at[2])
    drain(cross_landed, last_recv.at[0])
    for d in range(X - 1):
        crossed = crossed + cross_landed[d].astype(F32)
    reduced = (rhs_second - crossed).astype(BF16)

    scatter(1, reduced)
    ring_pass(2, (1,))
    for step in range(3, half):
        ring_pass(step)
    gather(1)
    ring_wait(half, 0, 0)
    update[...] = contract_rows(panels[0], trail_all[0].reshape(Z * bc, rows))
    gathered(1)
    spread_rows(1)

    ring_wait(half, 1, 1)
    second_turned = panels[1].T
    parts = 2
    part = rows // parts
    for index in range(parts):
        lanes = pl.ds(index * part, part)
        total = update[:, lanes] + contract(second_turned, trail_all[1, :, :, lanes].reshape(Z * bc, part))
        update[:, lanes] = total
        update_sent[index] = total.astype(BF16).reshape(X, share, part)
        for slot, d in enumerate(x_steps):
            send(update_sent.at[index, x_peer(d)], update_landed.at[index, slot], last_send.at[1 + index],
                 last_recv.at[1 + index], (row, x_peer(d) * Z + z))
    drain(first_rows.at[pl.ds(0, R - 1)], first_recv.at[2])
    write_rows(0, [
        jnp.concatenate([first_rows[index * sets + block % sets, block // sets].astype(F32) for index in range(slabs)], axis=0)
        for block in range(Z)
    ])
    for index in range(parts):
        lanes = pl.ds(index * part, part)
        total = update[pl.ds(pl.multiple_of(x * share, share), share), lanes]
        drain(update_landed.at[index], last_recv.at[1 + index])
        for slot in range(X - 1):
            total = total + update_landed[index, slot].astype(F32)
        new[:, lanes] = old[:, lanes] - total
    drain(rows_landed.at[pl.ds(0, Z - 1)], rows_recv.at[0])
    write_rows(1, [rows_landed[block].astype(F32) for block in range(Z)])

    drain(first_landed, first_send.at[0])
    drain(panels.at[0, pl.ds(0, (R - 1) * 2 * slab), :], first_send.at[1])
    for side in range(2):
        @pl.when(my_set + side * sets != z)
        def _():
            drain(first_piece.at[side], first_send.at[1])
    drain(first_rows.at[pl.ds(0, R - 1)], first_send.at[2])
    for buffer in (cross_all, diag_all):
        drain(buffer.at[pl.ds(0, Z - 1)], near_send.at[0])
    ring_drain()
    drain(landed, sum_send.at[0])
    drain(panels.at[1, pl.ds(0, (R - 1) * piece), :], sum_send.at[1])
    drain(rows_landed.at[pl.ds(0, Z - 1)], rows_send.at[0])
    drain(cross_landed, last_send.at[0])
    for index in range(parts):
        drain(update_landed.at[index], last_send.at[1 + index])


def build(mesh, X, Z):
    R = mesh.shape["row"]

    def per_device(panel_rhs, diag_inverse, cross_block, trail_factor, trail_rhs):
        _, br, nrhs = panel_rhs.shape
        bc = diag_inverse.shape[1]
        rows = trail_factor.shape[0]
        share = nrhs // (X * Z)
        width = share * X
        piece = Z * bc // R
        slab = bc // (R // (Z // 2))
        vmem = pl.BlockSpec(memory_space=pltpu.VMEM)
        solved, new = pl.pallas_call(
            functools.partial(kernel, R, X, Z),
            out_shape=(
                pltpu.VMEM((2, bc, nrhs), BF16),
                pltpu.VMEM((share, rows), F32),
            ),
            in_specs=[pl.BlockSpec(memory_space=pltpu.HBM)] * 5,
            out_specs=(vmem, vmem),
            scratch_shapes=[
                pltpu.VMEM((2, br, nrhs), BF16),
                pltpu.VMEM((share, rows), F32),
                pltpu.VMEM((2, Z, bc, rows), BF16),
                pltpu.VMEM((bc, br), BF16),
                pltpu.VMEM((Z, bc, br), BF16),
                pltpu.VMEM((Z, bc, br), BF16),
                pltpu.VMEM((Z * bc, width), F32),
                pltpu.VMEM((R, piece, width), BF16),
                pltpu.VMEM((R - 1, piece, width), BF16),
                pltpu.VMEM((2, Z * bc, width), BF16),
                pltpu.VMEM((br, width), BF16),
                pltpu.VMEM((X - 1, br, width), BF16),
                pltpu.VMEM((width, rows), F32),
                pltpu.VMEM((2, X, share, rows // 2), BF16),
                pltpu.VMEM((2, X - 1, share, rows // 2), BF16),
                pltpu.VMEM((Z, bc, width), BF16),
                pltpu.VMEM((br, Z * bc), BF16),
                pltpu.VMEM((R, 2, slab, width), BF16),
                pltpu.VMEM((R - 1, 2, slab, width), BF16),
                pltpu.VMEM((R, 2, slab, width), F32),
                pltpu.VMEM((2, slab, width), BF16),
                pltpu.VMEM((R, 2, slab, width), BF16),
                pltpu.SemaphoreType.DMA((6,)),
                pltpu.SemaphoreType.DMA((1,)),
                pltpu.SemaphoreType.DMA((3,)),
                pltpu.SemaphoreType.DMA((2, 2, Z // 2)),
                pltpu.SemaphoreType.DMA((2, 2, Z // 2)),
                pltpu.SemaphoreType.DMA((2,)),
                pltpu.SemaphoreType.DMA((2,)),
                pltpu.SemaphoreType.DMA((1,)),
                pltpu.SemaphoreType.DMA((1,)),
                pltpu.SemaphoreType.DMA((3,)),
                pltpu.SemaphoreType.DMA((3,)),
                pltpu.SemaphoreType.DMA((3,)),
                pltpu.SemaphoreType.DMA((3,)),
            ],
            compiler_params=pltpu.CompilerParams(
                collective_id=0, has_side_effects=True, vmem_limit_bytes=63 * 1024 * 1024
            ),
        )(
            panel_rhs,
            diag_inverse,
            cross_block.T,
            jnp.transpose(trail_factor, (1, 2, 0)),
            trail_rhs.T,
        )
        return solved, new.T

    in_specs = (
        P(None, "row", None),
        P(None, "col", "row"),
        P("row", "col"),
        P("row", None, "col"),
        P("row", "col"),
    )
    out_specs = (P(None, "col", None), P("row", "col"))
    return jax.shard_map(
        per_device, mesh=mesh, in_specs=in_specs, out_specs=out_specs, check_vma=False
    )


def solution(mesh):
    return build(mesh, 4, 8)
```
